32 devices in a mesh: expert: 8 (over y, x, core), tensor: 4 (over z).
Axes of the slice: x: 2, y: 2, z: 4, core: 2. Of those that a mesh axis runs over, the one named last changes fastest.
Arguments:
- tokens: bfloat16 [1024, 4096], P('expert', 'tensor'), may hold values from -6 to 6
- routes: int32 [1024, 2], P('expert'), may hold values from 0 to 7, all different within a row; in each aligned block of 128 rows (0 to 127, 128 to 255, ...) at most 64 rows name the same one
- route_gates: float32 [1024, 2], P('expert'), may hold values from 0.1 to 0.6
- gate_weight: bfloat16 [8, 4096, 2048], P('expert', None, 'tensor'), may hold values from -0.09375 to 0.09375
- up_weight: bfloat16 [8, 4096, 2048], P('expert', None, 'tensor'), may hold values from -0.09375 to 0.09375
- down_weight: bfloat16 [8, 2048, 4096], P('expert', 'tensor'), may hold values from -0.1875 to 0.1875
Outputs:
- combined: bfloat16 [1024, 4096], P('expert', 'tensor')
The draws below stay inside these ranges and needn't reach their ends.
Inputs may be any that keep to these rules, and one draw needn't show every extreme that they name: Within each aligned block of 128 tokens no expert is named by more than 64 routes, and the 2 experts of one token differ.
All inputs are finite; a program needn't handle non-finite values.
Results may differ from the reference program's by a relative error of at most 0.02.
Values may be sent and summed in bfloat16 or wider, within the bound.
No kernel may reach another device: no remote copies, remote signals or barrier semaphores. Data moves between devices by JAX's collectives and lax.ppermute only.
A program may use at most 64 MiB of HBM per device.

```python
import math
import jax
import jax.numpy as jnp
import numpy as np
from jax import lax

D = 4096
FF = 2048
ROUTES = 2
TOK_G = 128
EXPERTS = 8
CAP = 64
TOKENS = 1024
N_EXPERT = 8
N_TENSOR = 4


def raised(drawn, key, source, target, shards_of, factor):
    owner, partner = [(jnp.arange(drawn.shape[axis_at]) // (drawn.shape[axis_at] // shards_of)).reshape([-1 if axis == axis_at else 1 for axis in range(drawn.ndim)]) for axis_at in (source, target)]
    chosen = jax.random.permutation(key, shards_of)[partner]
    strong = (owner == chosen) | (owner == (partner + shards_of // 2) % shards_of)
    return jnp.where(strong, factor * drawn, drawn)


def steps_of(own_key, extent, pieces, low, largest):
    gain, own = 1.0, jax.random.fold_in(own_key, 6)
    for position, blocks in pieces:
        draws = jnp.exp(jax.random.uniform(jax.random.fold_in(own, position), (blocks,), jnp.float32, low / len(pieces), largest / len(pieces)))
        gain = gain * jnp.repeat(draws, extent[position] // blocks).reshape([-1 if axis == position else 1 for axis in range(len(extent))])
    return gain


def assign_block(key, own, number, rows, number_of, top, bound, skew):
    order = jax.random.permutation(key, number_of)
    crowded, ordinary = load_shares(number_of, rows * top, bound, skew, True), load_shares(number_of, rows * top, bound, skew, False)
    places = jnp.arange(number_of)

    def named(tallies, rotation):
        used = int((tallies > 0).sum())
        fixed = max(1, used // 4)
        passed = fixed + (places - fixed + rotation * (used - fixed)) % max(1, number_of - fixed)
        return jnp.zeros((number_of,), jnp.int32).at[order[jnp.where(places < fixed, places, passed)]].set(jnp.asarray(tallies, jnp.int32))

    tallies = jnp.where(number % 4 == 0, named(crowded, number // 4), named(ordinary, number - number // 4 - 1))
    mixed = jax.random.permutation(jax.random.fold_in(own, 3), number_of)
    giver, receiver = mixed[0:number_of // 2 * 2:2], mixed[1:number_of // 2 * 2:2]
    slack = jnp.minimum(tallies[giver] - 1, bound - tallies[receiver]) // 2
    slack = jnp.where((giver == order[0]) | (receiver == order[0]) | (tallies[receiver] == 0), 0, jnp.maximum(slack, 0))
    passed = jax.random.randint(jax.random.fold_in(own, 4), (number_of // 2,), 0, 1 << 20) % (slack + 1)
    tallies = tallies.at[giver].add(-passed).at[receiver].add(passed)
    members = jnp.searchsorted(jnp.cumsum(tallies), jnp.arange(rows * top), side="right").astype(jnp.int32)
    listing = members.reshape(top, rows).T
    listing = listing[jax.random.permutation(jax.random.fold_in(own, 1), rows)]
    rotation = jax.random.randint(jax.random.fold_in(own, 2), (rows, 1), 0, top)
    return jnp.take_along_axis(listing, (jnp.arange(top)[None, :] + rotation) % top, axis=1)


def load_shares(amount, total, most, lean, full):
    weights = [(1 << 20) // math.isqrt(grade ** lean) + 1 for grade in range(1, amount + 1)]
    largest = most if full else min(most, max(-(-total // amount), total * weights[0] // sum(weights)))
    least = 1 if total - largest >= amount - 1 else 0
    given, spare = [largest] + [least] * (amount - 1), total - largest - least * (amount - 1)
    while spare > 0:
        movable = [i for i in range(1, amount) if given[i] < largest] or [i for i in range(1, amount) if given[i] < most]
        whole, budget = sum([weights[i] for i in movable]), spare
        for i in movable:
            more = min(most - given[i], max(1, budget * weights[i] // whole), spare)
            given[i] = given[i] + more
            spare = spare - more
    return np.array(given)


def bell_draw(key, extent, spread, most, pieces=(), held_as=jnp.bfloat16):
    values = jax.random.normal(key, extent, jnp.float32) * spread
    if len(pieces) > 0:
        values = steps_of(key, extent, pieces, -0.22, 0.18) * values
    return jnp.clip(values, min=-most, max=most).astype(held_as)


def gaussian_with(stream_key, extent, deviation, reach, pieces, heavy, kind=jnp.bfloat16):
    values = deviation * jax.random.normal(stream_key, extent, jnp.float32)
    if pieces:
        values = values * steps_of(stream_key, extent, pieces, -0.22, 0.18)
    return jnp.clip(raised(values, jax.random.fold_in(stream_key, 3), *heavy), -reach, reach).astype(kind)


def setup_inputs(seed: int = 0) -> dict:
    key_of = jax.random.split(jax.random.key(seed), 7)
    tokens = bell_draw(key_of[0], (TOKENS, D), 1.0, 6.0, ((0, 8), (1, 4)))
    routes_keys = jax.random.split(jax.random.fold_in(key_of[1], 1), TOKENS // TOK_G)
    routes_turns = jax.random.permutation(jax.random.fold_in(key_of[1], 3), TOKENS // TOK_G)
    routes = jax.vmap(lambda own, number: assign_block(jax.random.fold_in(key_of[1], 2), own, number, TOK_G, EXPERTS, ROUTES, CAP, 2))(routes_keys, routes_turns).reshape((TOKENS, ROUTES))
    route_gates = jnp.clip(0.1 + 0.5 * jax.random.uniform(key_of[2], (TOKENS, ROUTES), jnp.float32) ** steps_of(key_of[2], (TOKENS, ROUTES), ((0, 8),), -0.2, 0.2), 0.1, 0.6)
    gate_weight = bell_draw(key_of[3], (EXPERTS, D, FF), D ** -0.5, 0.09375, ((0, 8), (2, 4)))
    up_weight = bell_draw(key_of[4], (EXPERTS, D, FF), D ** -0.5, 0.09375, ((0, 8), (2, 4)))
    down_weight = gaussian_with(key_of[5], (EXPERTS, FF, D), FF ** -0.5, 0.1875, ((0, 8), (1, 4)), (1, 2, 4, 2.0))
    return {"tokens": tokens, "routes": routes, "route_gates": route_gates, "gate_weight": gate_weight, "up_weight": up_weight, "down_weight": down_weight}


def reference(tokens, routes, route_gates, gate_weight, up_weight, down_weight):
    slot_total = N_EXPERT * CAP
    grouped = routes.reshape(N_EXPERT, TOK_G * ROUTES)
    onehot = (grouped[:, :, None] == jnp.arange(EXPERTS, dtype=jnp.int32)[None, None, :]).astype(jnp.int32)
    before = jnp.cumsum(onehot, axis=1) - onehot
    slot_ids = jnp.sum(before * onehot, axis=2).reshape(TOKENS, ROUTES).astype(jnp.int32)
    source_ids = (jnp.arange(TOKENS, dtype=jnp.int32) // TOK_G)[:, None]
    places = (source_ids * CAP + slot_ids).astype(jnp.int32)
    repeated = jnp.repeat(tokens, ROUTES, axis=0)

    def one_expert(expert):
        target = jnp.where(routes == expert, places, slot_total).reshape(-1).astype(jnp.int32)
        received = jnp.zeros((slot_total, D), jnp.bfloat16).at[target].set(repeated, mode="drop")
        gate_proj = jnp.dot(received, gate_weight[expert], preferred_element_type=jnp.float32)
        up_proj = jnp.dot(received, up_weight[expert], preferred_element_type=jnp.float32)
        hidden = (jax.nn.silu(gate_proj) * up_proj).astype(jnp.bfloat16)
        hidden_blocks = hidden.reshape(slot_total, N_TENSOR, FF // N_TENSOR).transpose(1, 0, 2)
        down_blocks = down_weight[expert].reshape(N_TENSOR, FF // N_TENSOR, D)

        def add_block(totals, pair):
            partial_value = jnp.dot(pair[0], pair[1], preferred_element_type=jnp.float32).astype(jnp.bfloat16)
            partial_value = lax.optimization_barrier(partial_value)
            return totals + partial_value.astype(jnp.float32), None

        summed, unused = lax.scan(add_block, jnp.zeros((slot_total, D), jnp.float32), (hidden_blocks, down_blocks))
        return summed.astype(jnp.bfloat16)

    expert_out = lax.map(one_expert, jnp.arange(EXPERTS, dtype=jnp.int32))
    flat_out = expert_out.reshape(EXPERTS * slot_total, D)
    lookup = (routes * slot_total + places).reshape(-1).astype(jnp.int32)
    picked = flat_out[lookup].astype(jnp.float32).reshape(TOKENS, ROUTES, D)
    combined = jnp.sum(picked * route_gates[:, :, None], axis=1)
    return combined.astype(jnp.bfloat16)
```

```python
import functools

import jax
import jax.numpy as jnp
from jax import lax
from jax.experimental import pallas as pl
from jax.experimental.pallas import tpu as pltpu
from jax.sharding import PartitionSpec as P

VMEM_BYTES = 40 * 1024 * 1024


def dispatch_plan(tokens, routes, route_gates, gate_weight, up_weight, down_weight):
    token_count = tokens.shape[0]
    slice_width = tokens.shape[1]
    route_count = routes.shape[1]
    source_count = lax.axis_size("expert")
    expert_count = gate_weight.shape[0] * source_count
    capacity = 2 * token_count * route_count // expert_count
    slot_total = source_count * capacity
    flat_routes = routes.reshape(-1)
    onehot = (flat_routes[:, None] == jnp.arange(expert_count, dtype=jnp.int32)[None, :]).astype(
        jnp.int32
    )
    before = jnp.cumsum(onehot, axis=0) - onehot
    slot_ids = jnp.sum(before * onehot, axis=1)
    places = flat_routes * capacity + slot_ids
    token_ids = jnp.arange(token_count * route_count, dtype=jnp.int32) // route_count
    outgoing = (
        jnp.zeros((expert_count * capacity, slice_width), jnp.bfloat16)
        .at[places]
        .set(tokens[token_ids])
    )
    outgoing = outgoing.reshape(expert_count, capacity, slice_width)
    arrived = lax.all_to_all(outgoing, "expert", split_axis=0, concat_axis=0, tiled=True)
    received = arrived.reshape(slot_total, slice_width)
    segment = lax.all_gather(received, "tensor", axis=1, tiled=True)
    gate_proj = jnp.dot(segment, gate_weight[0], preferred_element_type=jnp.float32)
    up_proj = jnp.dot(segment, up_weight[0], preferred_element_type=jnp.float32)
    hidden = (jax.nn.silu(gate_proj) * up_proj).astype(jnp.bfloat16)
    partial_value = lax.dot_general(
        down_weight[0], hidden, (((0,), (1,)), ((), ())), preferred_element_type=jnp.float32
    )
    summed = lax.psum_scatter(
        partial_value.astype(jnp.bfloat16), "tensor", scatter_dimension=0, tiled=True
    )
    expert_out = summed.reshape(slice_width, source_count, capacity)
    returned = lax.all_to_all(expert_out, "expert", split_axis=1, concat_axis=1, tiled=True)
    flat_back = returned.reshape(slice_width, expert_count * capacity)
    picked = jnp.take(flat_back, places, axis=1).astype(jnp.float32)
    weighted = picked * route_gates.reshape(-1)[None, :]
    combined = jnp.sum(weighted.reshape(slice_width, token_count, route_count), axis=2)
    return combined.T.astype(jnp.bfloat16)


def arrival(step):
    return step ^ (step >> 1)


def ffn_kernel(
    groups, blocks, splits, separate, place_ref, *refs
):
    x_refs = refs[: blocks * groups]
    coef_ref, gate0, up0, gate1, up1, down0, down1 = refs[blocks * groups : blocks * groups + 7]
    out_count = blocks if separate else groups
    out_refs = refs[blocks * groups + 7 : blocks * groups + 7 + out_count]
    x_all, totals, hidden, sems = refs[blocks * groups + 7 + out_count :]
    rows = x_refs[0].shape[0]
    depth = gate0.shape[0]
    half = gate0.shape[1]
    step = pl.program_id(0)
    inner = blocks * splits

    def copy(block, group):
        return pltpu.make_async_copy(
            x_refs[block * groups + group],
            x_all.at[block, pl.ds(group * rows, rows), :],
            sems.at[block, group],
        )

    @pl.when(step == 0)
    def _():
        for block in range(blocks):
            for group in range(groups):
                copy(block, group).start()
        totals[...] = jnp.zeros_like(totals)

    for block in range(blocks):

        @pl.when(step == block * splits)
        def _():
            for group in range(groups):
                copy(block, group).wait()

    @pl.when(step < inner)
    def _():
        columns = pl.ds(pl.multiple_of(lax.rem(step, splits) * depth, depth), depth)
        x = x_all[lax.div(step, splits), :, columns]
        for place, weight in enumerate((gate0, up0, gate1, up1)):
            totals[place] += jnp.dot(x, weight[...], preferred_element_type=jnp.float32)

    @pl.when(step == inner - 1)
    def _():
        for expert in range(2):
            gate = totals[2 * expert]
            value = gate / (1.0 + jnp.exp(-gate)) * totals[2 * expert + 1]
            hidden[:, expert * half : (expert + 1) * half] = (
                value * coef_ref[:, expert : expert + 1]
            ).astype(jnp.bfloat16)

    @pl.when(step >= inner)
    def _():
        part = jnp.dot(hidden[:, :half], down0[...], preferred_element_type=jnp.float32)
        part += jnp.dot(hidden[:, half:], down1[...], preferred_element_type=jnp.float32)
        part = part.astype(jnp.bfloat16)
        if separate:
            for block in range(blocks):

                @pl.when(step == inner + block)
                def _():
                    out_refs[block][...] = part
        else:
            for group in range(groups):
                out_refs[group][0] = part[group * rows : (group + 1) * rows]


def ffn(place, xs, coef, weights, separate):
    blocks, groups = len(xs), len(xs[0])
    rows, width = xs[0][0].shape
    half = weights[0].shape[1]
    splits = 2 if width % 256 == 0 else 1
    depth = width // splits
    inner = blocks * splits

    def into(step, place):
        now = jnp.minimum(step, inner - 1)
        source = lax.rem(place[0] - arrival(now // splits) + blocks, blocks)
        return source * splits + lax.rem(now, splits), 0

    def leaving(step):
        return jnp.maximum(step - inner, 0)

    def out_of(step, place):
        return 0, lax.rem(place[0] + arrival(blocks - 1 - leaving(step)), blocks)

    whole = lambda step, place: (0, 0)
    if separate:
        out_shape = [jax.ShapeDtypeStruct((groups * rows, width), jnp.bfloat16)] * blocks
        out_specs = [pl.BlockSpec((groups * rows, width), whole)] * blocks
    else:
        out_shape = [jax.ShapeDtypeStruct((blocks, rows, width), jnp.bfloat16)] * groups
        out_specs = [
            pl.BlockSpec((1, rows, width), lambda step, place: (leaving(step), 0, 0))
        ] * groups
    total_rows = groups * rows
    return pl.pallas_call(
        functools.partial(ffn_kernel, groups, blocks, splits, separate),
        out_shape=out_shape,
        grid_spec=pltpu.PrefetchScalarGridSpec(
            num_scalar_prefetch=1,
            grid=(inner + blocks,),
            in_specs=[pl.BlockSpec(memory_space=pl.ANY)] * (blocks * groups)
            + [pl.BlockSpec((total_rows, 2), whole)]
            + [pl.BlockSpec((depth, half), into)] * 4
            + [pl.BlockSpec((half, width), out_of)] * 2,
            out_specs=out_specs,
            scratch_shapes=[
                pltpu.VMEM((blocks, total_rows, width), jnp.bfloat16),
                pltpu.VMEM((4, total_rows, half), jnp.float32),
                pltpu.VMEM((total_rows, 2 * half), jnp.bfloat16),
                pltpu.SemaphoreType.DMA((blocks, groups)),
            ],
        ),
        compiler_params=pltpu.CompilerParams(vmem_limit_bytes=VMEM_BYTES),
        cost_estimate=pl.CostEstimate(
            flops=2 * total_rows * blocks * width * 6 * half,
            bytes_accessed=12 * blocks * width * half + 4 * blocks * total_rows * width,
            transcendentals=total_rows * 2 * half,
        ),
    )(place, *[x for block in xs for x in block], coef, *weights)


def after(value, *earlier):
    return lax.optimization_barrier((value,) + earlier)[0]


def gather_plan(tokens, routes, route_gates, gate_weight, up_weight, down_weight):
    devices = lax.axis_size("expert")
    depth = lax.axis_size("tensor")
    me = lax.axis_index("expert")
    place = lax.axis_index("tensor")
    wide = jnp.float32
    narrow = jnp.bfloat16

    def over(value, which):
        pairs = [(i, i ^ ((2, 4) if i % 2 == which else (4, 2))[0]) for i in range(devices)]
        return lax.ppermute(value, "expert", pairs)

    def near(value):
        return over(value, 0)

    def far(value):
        return over(value, 1)

    def twin(value):
        return lax.ppermute(value, "expert", [(i, i ^ 1) for i in range(devices)])

    def shift(value, by):
        return lax.ppermute(value, "tensor", [(i, (i + by) % depth) for i in range(depth)])

    named = routes[:, :, None] == jnp.arange(devices, dtype=jnp.int32)[None, None, :]
    coef = jnp.sum(jnp.where(named, route_gates[:, :, None], 0.0), axis=1)

    order = [arrival(i) for i in range(depth)]
    own = [tokens if by == 0 else shift(tokens, by) for by in order]
    a, b, g = [], [], []
    coef_a, coef_b = near(coef), far(coef)
    coef_g = near(coef_b)
    for block in own:
        a.append(near(block))
        b.append(far(block))
        g.append(near(b[-1]))

    mine = [gate_weight[0], up_weight[0], down_weight[0]]
    other = [twin(w) for w in mine]
    weights = [mine[0], mine[1], other[0], other[1], mine[2], other[2]]
    place = place.astype(jnp.int32).reshape(1)

    def gates_of(value):
        return jnp.concatenate(
            [
                lax.dynamic_slice_in_dim(value, me, 1, axis=1),
                lax.dynamic_slice_in_dim(value, me ^ 1, 1, axis=1),
            ],
            axis=1,
        )

    coef_main = gates_of(jnp.concatenate([coef, coef_a, coef_b], axis=0))
    main = [[own[i], a[i], b[i]] for i in range(depth)]
    y_own, y_a, y_b = ffn(place, main, coef_main, weights, False)
    y_g = ffn(place, [[v] for v in g], gates_of(coef_g), weights, True)

    from_a = near(y_a)
    result = None
    arrived = []
    for i in range(depth):
        by = order[depth - 1 - i]
        passed = near(y_g[i])
        send = (y_b[i].astype(wide) + passed.astype(wide)).astype(narrow)
        from_b = far(send)
        total = y_own[i].astype(wide) + from_a[i].astype(wide) + from_b.astype(wide)
        if by == 0:
            result = total
        else:
            arrived.append(shift(total.astype(narrow), by))
    for value in arrived:
        result = result + value.astype(wide)
    return result.astype(narrow)


def solution(mesh):
    small = mesh.shape["expert"] == 8 and mesh.shape["tensor"] == 4
    return jax.shard_map(
        gather_plan if small else dispatch_plan,
        mesh=mesh,
        in_specs=(
            P("expert", "tensor"),
            P("expert", None),
            P("expert", None),
            P("expert", None, "tensor"),
            P("expert", None, "tensor"),
            P("expert", "tensor", None),
        ),
        out_specs=P("expert", "tensor"),
        check_vma=False,
    )
```

```python
import functools

import jax
import jax.numpy as jnp
from jax import lax
from jax.experimental import pallas as pl
from jax.experimental.pallas import tpu as pltpu
from jax.sharding import PartitionSpec as P

VMEM_BYTES = 40 * 1024 * 1024


def dispatch_plan(tokens, routes, route_gates, gate_weight, up_weight, down_weight):
    token_count = tokens.shape[0]
    slice_width = tokens.shape[1]
    route_count = routes.shape[1]
    source_count = lax.axis_size("expert")
    expert_count = gate_weight.shape[0] * source_count
    capacity = 2 * token_count * route_count // expert_count
    slot_total = source_count * capacity
    flat_routes = routes.reshape(-1)
    onehot = (flat_routes[:, None] == jnp.arange(expert_count, dtype=jnp.int32)[None, :]).astype(
        jnp.int32
    )
    before = jnp.cumsum(onehot, axis=0) - onehot
    slot_ids = jnp.sum(before * onehot, axis=1)
    places = flat_routes * capacity + slot_ids
    token_ids = jnp.arange(token_count * route_count, dtype=jnp.int32) // route_count
    outgoing = (
        jnp.zeros((expert_count * capacity, slice_width), jnp.bfloat16)
        .at[places]
        .set(tokens[token_ids])
    )
    outgoing = outgoing.reshape(expert_count, capacity, slice_width)
    arrived = lax.all_to_all(outgoing, "expert", split_axis=0, concat_axis=0, tiled=True)
    received = arrived.reshape(slot_total, slice_width)
    segment = lax.all_gather(received, "tensor", axis=1, tiled=True)
    gate_proj = jnp.dot(segment, gate_weight[0], preferred_element_type=jnp.float32)
    up_proj = jnp.dot(segment, up_weight[0], preferred_element_type=jnp.float32)
    hidden = (jax.nn.silu(gate_proj) * up_proj).astype(jnp.bfloat16)
    partial_value = lax.dot_general(
        down_weight[0], hidden, (((0,), (1,)), ((), ())), preferred_element_type=jnp.float32
    )
    summed = lax.psum_scatter(
        partial_value.astype(jnp.bfloat16), "tensor", scatter_dimension=0, tiled=True
    )
    expert_out = summed.reshape(slice_width, source_count, capacity)
    returned = lax.all_to_all(expert_out, "expert", split_axis=1, concat_axis=1, tiled=True)
    flat_back = returned.reshape(slice_width, expert_count * capacity)
    picked = jnp.take(flat_back, places, axis=1).astype(jnp.float32)
    weighted = picked * route_gates.reshape(-1)[None, :]
    combined = jnp.sum(weighted.reshape(slice_width, token_count, route_count), axis=2)
    return combined.T.astype(jnp.bfloat16)


ANY = pl.BlockSpec(memory_space=pl.ANY)
HBM = pl.BlockSpec(memory_space=pltpu.HBM)
VMEM = pl.BlockSpec(memory_space=pltpu.VMEM)
SMEM = pl.BlockSpec(memory_space=pltpu.SMEM)


def limit(size):
    return pltpu.CompilerParams(vmem_limit_bytes=size * 1024 * 1024)


def x_copies(parts, x_refs, x_all, sems, width):
    copies = []
    for i, block in enumerate(parts):
        for group, (number, first) in enumerate(block):
            rows = x_all.shape[0] // len(block)
            copies.append(
                pltpu.make_async_copy(
                    x_refs[number].at[pl.ds(first, rows), pl.ds(0, width)],
                    x_all.at[pl.ds(group * rows, rows), pl.ds(i * width, width)],
                    sems.at[i, group],
                )
            )
    return copies


def w_copies(blocks, depth, place, refs, w_all, sems, width):
    copies = [[] for _ in range(4)]
    for i, block in enumerate(blocks):
        source = lax.rem(place - block + depth, depth)
        rows = pl.ds(pl.multiple_of(source * width, width), width)
        for k in range(4):
            origin = refs[k].at[rows, :]
            copies[k].append(
                pltpu.make_async_copy(
                    origin, w_all.at[k, pl.ds(i * width, width), :], sems.at[k, i]
                )
            )
    return copies


def project_kernel(depth, blocks, parts, arrays, place_ref, *refs):
    x_refs, refs = refs[:arrays], refs[arrays:]
    w_refs, refs = refs[:4], refs[4:]
    totals_refs, (x_all, w_all, x_sems, w_sems) = refs[:4], refs[4:]
    width = x_all.shape[1] // len(blocks)
    xs = x_copies(parts, x_refs, x_all, x_sems, width)
    ws = w_copies(blocks, depth, place_ref[0], w_refs, w_all, w_sems, width)
    for copy in xs + ws[0] + ws[1] + ws[2] + ws[3]:
        copy.start()
    for copy in xs:
        copy.wait()
    for k in range(4):
        for copy in ws[k]:
            copy.wait()
        totals_refs[k][...] = jnp.dot(
            x_all[...], w_all[k], preferred_element_type=jnp.float32
        )


def project(depth, place, blocks, arrays, parts, rows, width, weights):
    half = weights[0].shape[1]
    total = rows * len(parts[0])
    span = len(blocks) * width
    return pl.pallas_call(
        functools.partial(project_kernel, depth, blocks, parts, len(arrays)),
        out_shape=[jax.ShapeDtypeStruct((total, half), jnp.float32)] * 4,
        in_specs=[SMEM] + [ANY] * len(arrays) + [HBM] * 4,
        out_specs=[VMEM] * 4,
        scratch_shapes=[
            pltpu.VMEM((total, span), jnp.bfloat16),
            pltpu.VMEM((4, span, half), jnp.bfloat16),
            pltpu.SemaphoreType.DMA((len(blocks), len(parts[0]))),
            pltpu.SemaphoreType.DMA((4, len(blocks))),
        ],
        compiler_params=limit(28),
        cost_estimate=pl.CostEstimate(
            flops=8 * total * span * half,
            bytes_accessed=8 * span * half + 16 * total * half,
            transcendentals=0,
        ),
    )(place, *arrays, *weights)


def finish_kernel(depth, block, last, parts, arrays, place_ref, *refs):
    x_refs, refs = refs[:arrays], refs[arrays:]
    w_refs, down_refs, refs = refs[:4], refs[4:6], refs[6:]
    totals_refs, coef_ref, refs = refs[:4], refs[4], refs[5:]
    groups = len(parts[0])
    hidden_ref, y_refs, refs = refs[0], refs[1 : 1 + groups], refs[1 + groups :]
    x_all, w_all, d_all, x_sems, w_sems, d_sems = refs
    total, width = x_all.shape
    rows, half = total // groups, w_all.shape[2]
    place = place_ref[0]
    xs = x_copies(parts, x_refs, x_all, x_sems, width)
    ws = w_copies([block], depth, place, w_refs, w_all, w_sems, width)
    target = lax.rem(place + last, depth)
    ds = [
        pltpu.make_async_copy(
            down_refs[k].at[:, pl.ds(pl.multiple_of(target * width, width), width)],
            d_all.at[k],
            d_sems.at[k],
        )
        for k in range(2)
    ]
    for copy in xs + ws[0] + ws[1] + ws[2] + ws[3] + ds:
        copy.start()
    for copy in xs:
        copy.wait()
    for expert in range(2):
        for copy in ws[2 * expert] + ws[2 * expert + 1]:
            copy.wait()
        gate, up = [
            totals_refs[j][...]
            + jnp.dot(x_all[...], w_all[j], preferred_element_type=jnp.float32)
            for j in (2 * expert, 2 * expert + 1)
        ]
        value = gate / (1.0 + jnp.exp(-gate)) * up * coef_ref[:, expert : expert + 1]
        hidden_ref[:, expert * half : (expert + 1) * half] = value.astype(jnp.bfloat16)
    for copy in ds:
        copy.wait()
    y = jnp.dot(hidden_ref[:, :half], d_all[0], preferred_element_type=jnp.float32)
    y += jnp.dot(hidden_ref[:, half:], d_all[1], preferred_element_type=jnp.float32)
    y = y.astype(jnp.bfloat16)
    for group in range(groups):
        y_refs[group][...] = y[group * rows : (group + 1) * rows]


def finish(depth, place, block, last, arrays, parts, rows, width, weights, downs, totals, coef):
    half = weights[0].shape[1]
    groups = len(parts[0])
    total = groups * rows
    outs = pl.pallas_call(
        functools.partial(finish_kernel, depth, block, last, parts, len(arrays)),
        out_shape=[jax.ShapeDtypeStruct((total, 2 * half), jnp.bfloat16)]
        + [jax.ShapeDtypeStruct((rows, width), jnp.bfloat16)] * groups,
        in_specs=[SMEM] + [ANY] * len(arrays) + [HBM] * 6 + [VMEM] * 5,
        out_specs=[VMEM] * (1 + groups),
        scratch_shapes=[
            pltpu.VMEM((total, width), jnp.bfloat16),
            pltpu.VMEM((4, width, half), jnp.bfloat16),
            pltpu.VMEM((2, half, width), jnp.bfloat16),
            pltpu.SemaphoreType.DMA((1, groups)),
            pltpu.SemaphoreType.DMA((4, 1)),
            pltpu.SemaphoreType.DMA((2,)),
        ],
        compiler_params=limit(28),
        cost_estimate=pl.CostEstimate(
            flops=12 * total * width * half,
            bytes_accessed=12 * width * half + 16 * total * half,
            transcendentals=2 * total * half,
        ),
    )(place, *arrays, *weights, *downs, *totals, coef)
    return outs[0], outs[1:]


def descend_kernel(depth, blocks, groups, place_ref, hidden_ref, own_ref, other_ref, *refs):
    y_refs, (d_all, sems) = refs[: groups * len(blocks)], refs[groups * len(blocks) :]
    rows = hidden_ref.shape[0] // groups
    half, width = d_all.shape[2:]
    place = place_ref[0]
    copies = []
    for i, block in enumerate(blocks):
        target = lax.rem(place + block, depth)
        copies.append(
            [
                pltpu.make_async_copy(
                    ref.at[:, pl.ds(pl.multiple_of(target * width, width), width)],
                    d_all.at[i, k],
                    sems.at[i, k],
                )
                for k, ref in enumerate((own_ref, other_ref))
            ]
        )
    for pair in copies:
        for copy in pair:
            copy.start()
    for i, pair in enumerate(copies):
        for copy in pair:
            copy.wait()
        y = jnp.dot(hidden_ref[:, :half], d_all[i, 0], preferred_element_type=jnp.float32)
        y += jnp.dot(hidden_ref[:, half:], d_all[i, 1], preferred_element_type=jnp.float32)
        y = y.astype(jnp.bfloat16)
        for group in range(groups):
            y_refs[i * groups + group][...] = y[group * rows : (group + 1) * rows]


def descend(depth, place, blocks, groups, hidden, own, other):
    total = hidden.shape[0]
    rows = total // groups
    half = own.shape[0]
    width = own.shape[1] // depth
    outs = pl.pallas_call(
        functools.partial(descend_kernel, depth, blocks, groups),
        out_shape=[jax.ShapeDtypeStruct((rows, width), jnp.bfloat16)] * (groups * len(blocks)),
        in_specs=[SMEM, VMEM, HBM, HBM],
        out_specs=[VMEM] * (groups * len(blocks)),
        scratch_shapes=[
            pltpu.VMEM((len(blocks), 2, half, width), jnp.bfloat16),
            pltpu.SemaphoreType.DMA((len(blocks), 2)),
        ],
        compiler_params=limit(20),
        cost_estimate=pl.CostEstimate(
            flops=4 * total * len(blocks) * width * half,
            bytes_accessed=4 * len(blocks) * width * half + 2 * total * len(blocks) * width,
            transcendentals=0,
        ),
    )(place, hidden, own, other)
    return [outs[i * groups : (i + 1) * groups] for i in range(len(blocks))]


def after(value, *earlier):
    return lax.optimization_barrier((value,) + earlier)[0]


def fixed(value):
    return pltpu.with_memory_space_constraint(value, pltpu.HBM)


class Window:
    def __init__(self, size):
        self.size = size
        self.done = []

    def __call__(self, move, value, *earlier):
        if len(self.done) >= self.size:
            earlier += (self.done[-self.size],)
        self.done.append(move(after(value, *earlier) if earlier else value))
        return self.done[-1]


def gather_plan(tokens, routes, route_gates, gate_weight, up_weight, down_weight):
    devices = lax.axis_size("expert")
    depth = lax.axis_size("tensor")
    me = lax.axis_index("expert")
    spot = lax.axis_index("tensor").astype(jnp.int32)
    place = spot.reshape(1)
    wide, narrow = jnp.float32, jnp.bfloat16
    rows, width = tokens.shape

    def over(value, which):
        pairs = [(i, i ^ (2 if i % 2 == which else 4)) for i in range(devices)]
        return lax.ppermute(value, "expert", pairs)

    def near(value):
        return over(value, 0)

    def far(value):
        return over(value, 1)

    def twin(value):
        return lax.ppermute(value, "expert", [(i, i ^ 1) for i in range(devices)])

    def shift(by):
        pairs = [(i, (i + by) % depth) for i in range(depth)]
        return lambda value: lax.ppermute(value, "tensor", pairs)

    named = routes[:, :, None] == jnp.arange(devices, dtype=jnp.int32)[None, None, :]
    gates = jnp.sum(jnp.where(named, route_gates[:, :, None], 0.0), axis=1)
    high = gates.astype(narrow)
    rest = gates - high.astype(wide)
    middle = rest.astype(narrow)
    low = (rest - middle.astype(wide)).astype(narrow)
    extra = jnp.concatenate(
        [high, middle, low, jnp.zeros((rows, 128 - 3 * devices), narrow)], axis=1
    )
    marked = jnp.concatenate([tokens, extra], axis=1)

    plane, line = Window(3), Window(2)
    z1 = line(shift(1), tokens)
    z3 = line(shift(3), tokens)
    b0 = plane(far, marked)
    a0 = plane(near, marked)
    g0 = plane(near, b0)
    z13 = jnp.concatenate([z1, z3], axis=0)
    z2 = line(shift(1), z1)
    b13 = plane(far, z13)
    a13 = plane(near, z13)
    g1 = line(shift(1), g0)
    g3 = line(shift(3), g0)
    b2 = plane(far, z2)
    a2 = plane(near, z2)
    mine = [gate_weight[0], up_weight[0], down_weight[0]]
    other = [twin(mine[0]), twin(mine[1])]
    other.append(twin(after(mine[2], b13, *other)))
    weights = [fixed(w) for w in (mine[0], mine[1], other[0], other[1])]
    downs = [fixed(mine[2]), fixed(other[2])]
    arrays = [marked, a0, b0, g0, z13, a13, b13, g1, g3]
    parts = [
        [(4, 0), (5, 0), (6, 0), (7, 0)],
        [(4, rows), (5, rows), (6, rows), (8, 0)],
        [(0, 0), (1, 0), (2, 0), (3, 0)],
    ]
    totals = project(
        depth, place, [1, 3, 0], arrays, parts, rows, width, weights
    )
    g2 = plane(near, b2)

    def gates_of(value):
        parts = value[:, width : width + 3 * devices].astype(wide).reshape(rows, 3, devices)
        whole = jnp.sum(parts, axis=1)
        return jnp.concatenate(
            [
                lax.dynamic_slice_in_dim(whole, me, 1, axis=1),
                lax.dynamic_slice_in_dim(whole, me ^ 1, 1, axis=1),
            ],
            axis=1,
        )

    coef = jnp.concatenate([gates_of(v) for v in (marked, a0, b0, g0)], axis=0)
    hidden, y2 = finish(
        depth, place, 2, 2, [z2, a2, b2, g2], [[(i, 0) for i in range(4)]], rows, width,
        weights, downs, totals, coef,
    )
    y = {2: y2}
    late = [1, 3, 0]
    for d, part in zip(late, descend(depth, place, late, 4, hidden, *downs)):
        y[d] = part

    def plus(*values):
        total = values[0].astype(wide)
        for value in values[1:]:
            total = total + value.astype(wide)
        return total

    plane, line = Window(3), Window(2)
    pg2 = plane(near, y[2][3])
    pa2 = plane(near, y[2][1])
    zg1 = line(shift(1), y[1][3])
    zg3 = line(shift(3), y[3][3])
    pb2 = plane(far, plus(y[2][2], pg2).astype(narrow))
    pa1 = plane(near, y[1][1])
    pb1 = plane(far, y[1][2])
    t2 = line(shift(1), plus(y[2][0], pa2, pb2).astype(narrow))
    pa3 = plane(near, y[3][1])
    pg0 = plane(near, plus(y[0][3], zg1, zg3).astype(narrow))
    pb3 = plane(far, y[3][2])
    t1 = line(shift(1), plus(y[1][0], pa1, pb1, t2).astype(narrow))
    pa0 = plane(near, y[0][1])
    pb0 = plane(far, plus(y[0][2], pg0).astype(narrow))
    t3 = line(shift(3), plus(y[3][0], pa3, pb3).astype(narrow))
    return plus(y[0][0], pa0, pb0, t1, t3).astype(narrow)


def solution(mesh):
    small = mesh.shape["expert"] == 8 and mesh.shape["tensor"] == 4
    return jax.shard_map(
        gather_plan if small else dispatch_plan,
        mesh=mesh,
        in_specs=(
            P("expert", "tensor"),
            P("expert", None),
            P("expert", None),
            P("expert", None, "tensor"),
            P("expert", None, "tensor"),
            P("expert", "tensor", None),
        ),
        out_specs=P("expert", "tensor"),
        check_vma=False,
    )
```

```python
import functools

import jax
import jax.numpy as jnp
from jax import lax
from jax.experimental import pallas as pl
from jax.experimental.pallas import tpu as pltpu
from jax.sharding import PartitionSpec as P

VMEM_BYTES = 40 * 1024 * 1024


def dispatch_plan(tokens, routes, route_gates, gate_weight, up_weight, down_weight):
    token_count = tokens.shape[0]
    slice_width = tokens.shape[1]
    route_count = routes.shape[1]
    source_count = lax.axis_size("expert")
    expert_count = gate_weight.shape[0] * source_count
    capacity = 2 * token_count * route_count // expert_count
    slot_total = source_count * capacity
    flat_routes = routes.reshape(-1)
    onehot = (flat_routes[:, None] == jnp.arange(expert_count, dtype=jnp.int32)[None, :]).astype(
        jnp.int32
    )
    before = jnp.cumsum(onehot, axis=0) - onehot
    slot_ids = jnp.sum(before * onehot, axis=1)
    places = flat_routes * capacity + slot_ids
    token_ids = jnp.arange(token_count * route_count, dtype=jnp.int32) // route_count
    outgoing = (
        jnp.zeros((expert_count * capacity, slice_width), jnp.bfloat16)
        .at[places]
        .set(tokens[token_ids])
    )
    outgoing = outgoing.reshape(expert_count, capacity, slice_width)
    arrived = lax.all_to_all(outgoing, "expert", split_axis=0, concat_axis=0, tiled=True)
    received = arrived.reshape(slot_total, slice_width)
    segment = lax.all_gather(received, "tensor", axis=1, tiled=True)
    gate_proj = jnp.dot(segment, gate_weight[0], preferred_element_type=jnp.float32)
    up_proj = jnp.dot(segment, up_weight[0], preferred_element_type=jnp.float32)
    hidden = (jax.nn.silu(gate_proj) * up_proj).astype(jnp.bfloat16)
    partial_value = lax.dot_general(
        down_weight[0], hidden, (((0,), (1,)), ((), ())), preferred_element_type=jnp.float32
    )
    summed = lax.psum_scatter(
        partial_value.astype(jnp.bfloat16), "tensor", scatter_dimension=0, tiled=True
    )
    expert_out = summed.reshape(slice_width, source_count, capacity)
    returned = lax.all_to_all(expert_out, "expert", split_axis=1, concat_axis=1, tiled=True)
    flat_back = returned.reshape(slice_width, expert_count * capacity)
    picked = jnp.take(flat_back, places, axis=1).astype(jnp.float32)
    weighted = picked * route_gates.reshape(-1)[None, :]
    combined = jnp.sum(weighted.reshape(slice_width, token_count, route_count), axis=2)
    return combined.T.astype(jnp.bfloat16)


ANY = pl.BlockSpec(memory_space=pl.ANY)
HBM = pl.BlockSpec(memory_space=pltpu.HBM)
VMEM = pl.BlockSpec(memory_space=pltpu.VMEM)
SMEM = pl.BlockSpec(memory_space=pltpu.SMEM)


def limit(size):
    return pltpu.CompilerParams(vmem_limit_bytes=size * 1024 * 1024)


def x_copies(parts, x_refs, x_all, sems, width):
    copies = []
    for i, block in enumerate(parts):
        for group, (number, first) in enumerate(block):
            rows = x_all.shape[0] // len(block)
            copies.append(
                pltpu.make_async_copy(
                    x_refs[number].at[pl.ds(first, rows), pl.ds(0, width)],
                    x_all.at[pl.ds(group * rows, rows), pl.ds(i * width, width)],
                    sems.at[i, group],
                )
            )
    return copies


def w_copies(blocks, depth, place, refs, w_all, sems, width):
    copies = [[] for _ in range(4)]
    for i, block in enumerate(blocks):
        source = lax.rem(place - block + depth, depth)
        rows = pl.ds(pl.multiple_of(source * width, width), width)
        for k in range(4):
            origin = refs[k].at[rows, :]
            copies[k].append(
                pltpu.make_async_copy(
                    origin, w_all.at[k, pl.ds(i * width, width), :], sems.at[k, i]
                )
            )
    return copies


def project_kernel(depth, blocks, parts, arrays, place_ref, *refs):
    x_refs, refs = refs[:arrays], refs[arrays:]
    w_refs, refs = refs[:4], refs[4:]
    totals_refs, (x_all, w_all, x_sems, w_sems) = refs[:4], refs[4:]
    width = x_all.shape[1] // len(blocks)
    xs = x_copies(parts, x_refs, x_all, x_sems, width)
    ws = w_copies(blocks, depth, place_ref[0], w_refs, w_all, w_sems, width)
    for copy in xs + ws[0] + ws[1] + ws[2] + ws[3]:
        copy.start()
    for copy in xs:
        copy.wait()
    for k in range(4):
        for copy in ws[k]:
            copy.wait()
        totals_refs[k][...] = jnp.dot(
            x_all[...], w_all[k], preferred_element_type=jnp.float32
        )


def project(depth, place, blocks, arrays, parts, rows, width, weights):
    half = weights[0].shape[1]
    total = rows * len(parts[0])
    span = len(blocks) * width
    return pl.pallas_call(
        functools.partial(project_kernel, depth, blocks, parts, len(arrays)),
        out_shape=[jax.ShapeDtypeStruct((total, half), jnp.float32)] * 4,
        in_specs=[SMEM] + [ANY] * len(arrays) + [HBM] * 4,
        out_specs=[VMEM] * 4,
        scratch_shapes=[
            pltpu.VMEM((total, span), jnp.bfloat16),
            pltpu.VMEM((4, span, half), jnp.bfloat16),
            pltpu.SemaphoreType.DMA((len(blocks), len(parts[0]))),
            pltpu.SemaphoreType.DMA((4, len(blocks))),
        ],
        compiler_params=limit(28),
        cost_estimate=pl.CostEstimate(
            flops=8 * total * span * half,
            bytes_accessed=8 * span * half + 16 * total * half,
            transcendentals=0,
        ),
    )(place, *arrays, *weights)


def finish_kernel(depth, block, last, parts, arrays, place_ref, *refs):
    x_refs, refs = refs[:arrays], refs[arrays:]
    w_refs, down_refs, refs = refs[:4], refs[4:6], refs[6:]
    totals_refs, coef_ref, refs = refs[:4], refs[4], refs[5:]
    groups = len(parts[0])
    hidden_ref, y_refs, refs = refs[0], refs[1 : 1 + groups], refs[1 + groups :]
    x_all, w_all, d_all, x_sems, w_sems, d_sems = refs
    total, width = x_all.shape
    rows, half = total // groups, w_all.shape[2]
    place = place_ref[0]
    xs = x_copies(parts, x_refs, x_all, x_sems, width)
    ws = w_copies([block], depth, place, w_refs, w_all, w_sems, width)
    target = lax.rem(place + last, depth)
    ds = [
        pltpu.make_async_copy(
            down_refs[k].at[:, pl.ds(pl.multiple_of(target * width, width), width)],
            d_all.at[k],
            d_sems.at[k],
        )
        for k in range(2)
    ]
    for copy in xs + ws[0] + ws[1] + ws[2] + ws[3] + ds:
        copy.start()
    for copy in xs:
        copy.wait()
    for expert in range(2):
        for copy in ws[2 * expert] + ws[2 * expert + 1]:
            copy.wait()
        gate, up = [
            totals_refs[j][...]
            + jnp.dot(x_all[...], w_all[j], preferred_element_type=jnp.float32)
            for j in (2 * expert, 2 * expert + 1)
        ]
        value = gate / (1.0 + jnp.exp(-gate)) * up * coef_ref[:, expert : expert + 1]
        hidden_ref[:, expert * half : (expert + 1) * half] = value.astype(jnp.bfloat16)
    for copy in ds:
        copy.wait()
    y = jnp.dot(hidden_ref[:, :half], d_all[0], preferred_element_type=jnp.float32)
    y += jnp.dot(hidden_ref[:, half:], d_all[1], preferred_element_type=jnp.float32)
    y = y.astype(jnp.bfloat16)
    for group in range(groups):
        y_refs[group][...] = y[group * rows : (group + 1) * rows]


def finish(depth, place, block, last, arrays, parts, rows, width, weights, downs, totals, coef):
    half = weights[0].shape[1]
    groups = len(parts[0])
    total = groups * rows
    outs = pl.pallas_call(
        functools.partial(finish_kernel, depth, block, last, parts, len(arrays)),
        out_shape=[jax.ShapeDtypeStruct((total, 2 * half), jnp.bfloat16)]
        + [jax.ShapeDtypeStruct((rows, width), jnp.bfloat16)] * groups,
        in_specs=[SMEM] + [ANY] * len(arrays) + [HBM] * 6 + [VMEM] * 5,
        out_specs=[VMEM] * (1 + groups),
        scratch_shapes=[
            pltpu.VMEM((total, width), jnp.bfloat16),
            pltpu.VMEM((4, width, half), jnp.bfloat16),
            pltpu.VMEM((2, half, width), jnp.bfloat16),
            pltpu.SemaphoreType.DMA((1, groups)),
            pltpu.SemaphoreType.DMA((4, 1)),
            pltpu.SemaphoreType.DMA((2,)),
        ],
        compiler_params=limit(28),
        cost_estimate=pl.CostEstimate(
            flops=12 * total * width * half,
            bytes_accessed=12 * width * half + 16 * total * half,
            transcendentals=2 * total * half,
        ),
    )(place, *arrays, *weights, *downs, *totals, coef)
    return outs[0], outs[1:]


def descend_kernel(depth, blocks, groups, place_ref, hidden_ref, own_ref, other_ref, *refs):
    y_refs, (d_all, sems) = refs[: groups * len(blocks)], refs[groups * len(blocks) :]
    rows = hidden_ref.shape[0] // groups
    half, width = d_all.shape[2:]
    place = place_ref[0]
    copies = []
    for i, block in enumerate(blocks):
        target = lax.rem(place + block, depth)
        copies.append(
            [
                pltpu.make_async_copy(
                    ref.at[:, pl.ds(pl.multiple_of(target * width, width), width)],
                    d_all.at[i, k],
                    sems.at[i, k],
                )
                for k, ref in enumerate((own_ref, other_ref))
            ]
        )
    for pair in copies:
        for copy in pair:
            copy.start()
    for i, pair in enumerate(copies):
        for copy in pair:
            copy.wait()
        y = jnp.dot(hidden_ref[:, :half], d_all[i, 0], preferred_element_type=jnp.float32)
        y += jnp.dot(hidden_ref[:, half:], d_all[i, 1], preferred_element_type=jnp.float32)
        y = y.astype(jnp.bfloat16)
        for group in range(groups):
            y_refs[i * groups + group][...] = y[group * rows : (group + 1) * rows]


def descend(depth, place, blocks, groups, hidden, own, other):
    total = hidden.shape[0]
    rows = total // groups
    half = own.shape[0]
    width = own.shape[1] // depth
    outs = pl.pallas_call(
        functools.partial(descend_kernel, depth, blocks, groups),
        out_shape=[jax.ShapeDtypeStruct((rows, width), jnp.bfloat16)] * (groups * len(blocks)),
        in_specs=[SMEM, VMEM, HBM, HBM],
        out_specs=[VMEM] * (groups * len(blocks)),
        scratch_shapes=[
            pltpu.VMEM((len(blocks), 2, half, width), jnp.bfloat16),
            pltpu.SemaphoreType.DMA((len(blocks), 2)),
        ],
        compiler_params=limit(20),
        cost_estimate=pl.CostEstimate(
            flops=4 * total * len(blocks) * width * half,
            bytes_accessed=4 * len(blocks) * width * half + 2 * total * len(blocks) * width,
            transcendentals=0,
        ),
    )(place, hidden, own, other)
    return [outs[i * groups : (i + 1) * groups] for i in range(len(blocks))]


def after(value, *earlier):
    return lax.optimization_barrier((value,) + earlier)[0]


def fixed(value):
    return pltpu.with_memory_space_constraint(value, pltpu.HBM)


class Window:
    def __init__(self, size):
        self.size = size
        self.done = []

    def __call__(self, move, value, *earlier):
        if len(self.done) >= self.size:
            earlier += (self.done[-self.size],)
        self.done.append(move(after(value, *earlier) if earlier else value))
        return self.done[-1]


def gather_plan(tokens, routes, route_gates, gate_weight, up_weight, down_weight):
    devices = lax.axis_size("expert")
    depth = lax.axis_size("tensor")
    me = lax.axis_index("expert")
    spot = lax.axis_index("tensor").astype(jnp.int32)
    place = spot.reshape(1)
    wide, narrow = jnp.float32, jnp.bfloat16
    rows, width = tokens.shape

    def over(value, which):
        pairs = [(i, i ^ (2 if i % 2 == which else 4)) for i in range(devices)]
        return lax.ppermute(value, "expert", pairs)

    def near(value):
        return over(value, 0)

    def far(value):
        return over(value, 1)

    def twin(value):
        return lax.ppermute(value, "expert", [(i, i ^ 1) for i in range(devices)])

    def shift(by):
        pairs = [(i, (i + by) % depth) for i in range(depth)]
        return lambda value: lax.ppermute(value, "tensor", pairs)

    named = routes[:, :, None] == jnp.arange(devices, dtype=jnp.int32)[None, None, :]
    gates = jnp.sum(jnp.where(named, route_gates[:, :, None], 0.0), axis=1)
    high = gates.astype(narrow)
    rest = gates - high.astype(wide)
    middle = rest.astype(narrow)
    low = (rest - middle.astype(wide)).astype(narrow)
    extra = jnp.concatenate(
        [high, middle, low, jnp.zeros((rows, 128 - 3 * devices), narrow)], axis=1
    )
    marked = jnp.concatenate([tokens, extra], axis=1)

    plane, line = Window(3), Window(2)
    mine = [gate_weight[0], up_weight[0], down_weight[0]]
    other = [twin(w) for w in mine]
    z1 = shift(1)(tokens)
    b0 = far(marked)
    g0 = near(b0)
    a0 = near(after(marked, g0))
    z3 = shift(3)(after(tokens, g0))
    z13 = after(jnp.concatenate([z1, z3], axis=0), a0, *other)
    b13 = far(z13)
    a13 = near(z13)
    z2 = shift(1)(after(z1, a0, *other))
    g1 = shift(1)(after(g0, a0, *other))
    g3 = shift(3)(after(g0, a0, *other))
    b2 = far(z2)
    a2 = near(z2)
    weights = [fixed(w) for w in (mine[0], mine[1], other[0], other[1])]
    downs = [fixed(mine[2]), fixed(other[2])]
    arrays = [marked, a0, b0, g0, z13, a13, b13, g1, g3]
    parts = [
        [(4, 0), (5, 0), (6, 0), (7, 0)],
        [(4, rows), (5, rows), (6, rows), (8, 0)],
        [(0, 0), (1, 0), (2, 0), (3, 0)],
    ]
    totals = project(
        depth, place, [1, 3, 0], arrays, parts, rows, width, weights
    )
    g2 = near(b2)

    def gates_of(value):
        parts = value[:, width : width + 3 * devices].astype(wide).reshape(rows, 3, devices)
        whole = jnp.sum(parts, axis=1)
        return jnp.concatenate(
            [
                lax.dynamic_slice_in_dim(whole, me, 1, axis=1),
                lax.dynamic_slice_in_dim(whole, me ^ 1, 1, axis=1),
            ],
            axis=1,
        )

    coef = jnp.concatenate([gates_of(v) for v in (marked, a0, b0, g0)], axis=0)
    hidden, y2 = finish(
        depth, place, 2, 2, [z2, a2, b2, g2], [[(i, 0) for i in range(4)]], rows, width,
        weights, downs, totals, coef,
    )
    y = {2: y2}
    late = [1, 3, 0]
    for d, part in zip(late, descend(depth, place, late, 4, hidden, *downs)):
        y[d] = part

    def plus(*values):
        total = values[0].astype(wide)
        for value in values[1:]:
            total = total + value.astype(wide)
        return total

    plane, line = Window(3), Window(2)
    pg2 = near(y[2][3])
    pa2 = near(y[2][1])
    zg1 = shift(1)(y[1][3])
    zg3 = shift(3)(y[3][3])
    pb2 = far(plus(y[2][2], pg2).astype(narrow))
    pa1 = near(y[1][1])
    pb1 = far(y[1][2])
    u2 = shift(1)(plus(y[2][0], pa2, pb2).astype(narrow))
    pa3 = near(after(y[3][1], pa2))
    pb3 = far(after(y[3][2], pb2))
    pg0 = near(plus(y[0][3], zg1, zg3).astype(narrow))
    pa0 = near(after(y[0][1], pg0))
    pb0 = far(plus(y[0][2], pg0).astype(narrow))
    t1 = shift(1)(plus(y[1][0], pa1, pb1, u2).astype(narrow))
    t3 = shift(3)(plus(y[3][0], pa3, pb3).astype(narrow))
    return plus(y[0][0], pa0, pb0, t1, t3).astype(narrow)


def solution(mesh):
    small = mesh.shape["expert"] == 8 and mesh.shape["tensor"] == 4
    return jax.shard_map(
        gather_plan if small else dispatch_plan,
        mesh=mesh,
        in_specs=(
            P("expert", "tensor"),
            P("expert", None),
            P("expert", None),
            P("expert", None, "tensor"),
            P("expert", None, "tensor"),
            P("expert", "tensor", None),
        ),
        out_specs=P("expert", "tensor"),
        check_vma=False,
    )
```

```python
import functools

import jax
import jax.numpy as jnp
from jax import lax
from jax.experimental import pallas as pl
from jax.experimental.pallas import tpu as pltpu
from jax.sharding import PartitionSpec as P

VMEM_BYTES = 40 * 1024 * 1024


def dispatch_plan(tokens, routes, route_gates, gate_weight, up_weight, down_weight):
    token_count = tokens.shape[0]
    slice_width = tokens.shape[1]
    route_count = routes.shape[1]
    source_count = lax.axis_size("expert")
    expert_count = gate_weight.shape[0] * source_count
    capacity = 2 * token_count * route_count // expert_count
    slot_total = source_count * capacity
    flat_routes = routes.reshape(-1)
    onehot = (flat_routes[:, None] == jnp.arange(expert_count, dtype=jnp.int32)[None, :]).astype(
        jnp.int32
    )
    before = jnp.cumsum(onehot, axis=0) - onehot
    slot_ids = jnp.sum(before * onehot, axis=1)
    places = flat_routes * capacity + slot_ids
    token_ids = jnp.arange(token_count * route_count, dtype=jnp.int32) // route_count
    outgoing = (
        jnp.zeros((expert_count * capacity, slice_width), jnp.bfloat16)
        .at[places]
        .set(tokens[token_ids])
    )
    outgoing = outgoing.reshape(expert_count, capacity, slice_width)
    arrived = lax.all_to_all(outgoing, "expert", split_axis=0, concat_axis=0, tiled=True)
    received = arrived.reshape(slot_total, slice_width)
    segment = lax.all_gather(received, "tensor", axis=1, tiled=True)
    gate_proj = jnp.dot(segment, gate_weight[0], preferred_element_type=jnp.float32)
    up_proj = jnp.dot(segment, up_weight[0], preferred_element_type=jnp.float32)
    hidden = (jax.nn.silu(gate_proj) * up_proj).astype(jnp.bfloat16)
    partial_value = lax.dot_general(
        down_weight[0], hidden, (((0,), (1,)), ((), ())), preferred_element_type=jnp.float32
    )
    summed = lax.psum_scatter(
        partial_value.astype(jnp.bfloat16), "tensor", scatter_dimension=0, tiled=True
    )
    expert_out = summed.reshape(slice_width, source_count, capacity)
    returned = lax.all_to_all(expert_out, "expert", split_axis=1, concat_axis=1, tiled=True)
    flat_back = returned.reshape(slice_width, expert_count * capacity)
    picked = jnp.take(flat_back, places, axis=1).astype(jnp.float32)
    weighted = picked * route_gates.reshape(-1)[None, :]
    combined = jnp.sum(weighted.reshape(slice_width, token_count, route_count), axis=2)
    return combined.T.astype(jnp.bfloat16)


ANY = pl.BlockSpec(memory_space=pl.ANY)
HBM = pl.BlockSpec(memory_space=pltpu.HBM)
VMEM = pl.BlockSpec(memory_space=pltpu.VMEM)
SMEM = pl.BlockSpec(memory_space=pltpu.SMEM)


def limit(size):
    return pltpu.CompilerParams(vmem_limit_bytes=size * 1024 * 1024)


def x_copies(parts, x_refs, x_all, sems, width):
    copies = []
    for i, block in enumerate(parts):
        for group, (number, first) in enumerate(block):
            rows = x_all.shape[0] // len(block)
            copies.append(
                pltpu.make_async_copy(
                    x_refs[number].at[pl.ds(first, rows), pl.ds(0, width)],
                    x_all.at[pl.ds(group * rows, rows), pl.ds(i * width, width)],
                    sems.at[i, group],
                )
            )
    return copies


def w_copies(blocks, depth, place, refs, w_all, sems, width):
    copies = [[] for _ in range(4)]
    for i, block in enumerate(blocks):
        source = lax.rem(place - block + depth, depth)
        rows = pl.ds(pl.multiple_of(source * width, width), width)
        for k in range(4):
            origin = refs[k].at[rows, :]
            copies[k].append(
                pltpu.make_async_copy(
                    origin, w_all.at[k, pl.ds(i * width, width), :], sems.at[k, i]
                )
            )
    return copies


def pick(x_all, picks_ref, xc_all, groups, columns):
    rows = x_all.shape[0] // groups
    slots = picks_ref.shape[1] // 2
    for group in range(groups):
        x = x_all[pl.ds(group * rows, rows), columns]
        z = jnp.dot(picks_ref[group], x, preferred_element_type=jnp.float32)
        z = z.astype(jnp.bfloat16)
        for expert in range(2):
            xc_all[expert, pl.ds(group * slots, slots), columns] = z[
                expert * slots : (expert + 1) * slots
            ]


def project_kernel(depth, blocks, parts, arrays, place_ref, *refs):
    x_refs, refs = refs[:arrays], refs[arrays:]
    w_refs, picks_ref, refs = refs[:4], refs[4], refs[5:]
    totals_refs, (x_all, xc_all, w_all, x_sems, w_sems) = refs[:4], refs[4:]
    groups = len(parts[0])
    width = x_all.shape[1] // len(blocks)
    xs = x_copies(parts, x_refs, x_all, x_sems, width)
    ws = w_copies(blocks, depth, place_ref[0], w_refs, w_all, w_sems, width)
    for copy in xs + ws[0] + ws[1] + ws[2] + ws[3]:
        copy.start()
    for i in range(len(blocks)):
        for copy in xs[i * groups : (i + 1) * groups]:
            copy.wait()
        pick(x_all, picks_ref, xc_all, groups, pl.ds(i * width, width))
    for k in range(4):
        for copy in ws[k]:
            copy.wait()
        totals_refs[k][...] = jnp.dot(
            xc_all[k // 2], w_all[k], preferred_element_type=jnp.float32
        )


def project(depth, place, blocks, arrays, parts, rows, width, weights, picks):
    half = weights[0].shape[1]
    groups = len(parts[0])
    total = rows * groups
    slots = groups * picks.shape[1] // 2
    span = len(blocks) * width
    return pl.pallas_call(
        functools.partial(project_kernel, depth, blocks, parts, len(arrays)),
        out_shape=[jax.ShapeDtypeStruct((slots, half), jnp.float32)] * 4,
        in_specs=[SMEM] + [ANY] * len(arrays) + [HBM] * 4 + [VMEM],
        out_specs=[VMEM] * 4,
        scratch_shapes=[
            pltpu.VMEM((total, span), jnp.bfloat16),
            pltpu.VMEM((2, slots, span), jnp.bfloat16),
            pltpu.VMEM((4, span, half), jnp.bfloat16),
            pltpu.SemaphoreType.DMA((len(blocks), groups)),
            pltpu.SemaphoreType.DMA((4, len(blocks))),
        ],
        compiler_params=limit(28),
        cost_estimate=pl.CostEstimate(
            flops=8 * total * span * half,
            bytes_accessed=8 * span * half + 16 * total * half,
            transcendentals=0,
        ),
    )(place, *arrays, *weights, picks)


def spread(hidden_ref, downs, places_ref, groups, put):
    slots = hidden_ref.shape[1] // groups
    each = [
        jnp.dot(hidden_ref[expert], downs[expert], preferred_element_type=jnp.float32).astype(
            jnp.bfloat16
        )
        for expert in range(2)
    ]
    for group in range(groups):
        part = slice(group * slots, (group + 1) * slots)
        both = jnp.concatenate([each[0][part], each[1][part]], axis=0)
        y = jnp.dot(places_ref[group], both, preferred_element_type=jnp.float32)
        put(group, y.astype(jnp.bfloat16))


def finish_kernel(depth, block, last, parts, arrays, place_ref, *refs):
    x_refs, refs = refs[:arrays], refs[arrays:]
    w_refs, down_refs, refs = refs[:4], refs[4:6], refs[6:]
    totals_refs, coef_ref, picks_ref, places_ref, refs = refs[:4], *refs[4:7], refs[7:]
    groups = len(parts[0])
    hidden_ref, y_refs, refs = refs[0], refs[1 : 1 + groups], refs[1 + groups :]
    x_all, xc_all, w_all, d_all, x_sems, w_sems, d_sems = refs
    width = x_all.shape[1]
    place = place_ref[0]
    xs = x_copies(parts, x_refs, x_all, x_sems, width)
    ws = w_copies([block], depth, place, w_refs, w_all, w_sems, width)
    target = lax.rem(place + last, depth)
    ds = [
        pltpu.make_async_copy(
            down_refs[k].at[:, pl.ds(pl.multiple_of(target * width, width), width)],
            d_all.at[k],
            d_sems.at[k],
        )
        for k in range(2)
    ]
    for copy in xs + ws[0] + ws[1] + ws[2] + ws[3] + ds:
        copy.start()
    for copy in xs:
        copy.wait()
    pick(x_all, picks_ref, xc_all, groups, pl.ds(0, width))
    for expert in range(2):
        for copy in ws[2 * expert] + ws[2 * expert + 1]:
            copy.wait()
        gate, up = [
            totals_refs[j][...]
            + jnp.dot(xc_all[expert], w_all[j], preferred_element_type=jnp.float32)
            for j in (2 * expert, 2 * expert + 1)
        ]
        value = gate / (1.0 + jnp.exp(-gate)) * up * coef_ref[:, expert : expert + 1]
        hidden_ref[expert] = value.astype(jnp.bfloat16)
    for copy in ds:
        copy.wait()

    def put(group, y):
        y_refs[group][...] = y

    spread(hidden_ref, d_all, places_ref, groups, put)


def finish(
    depth, place, block, last, arrays, parts, rows, width, weights, downs, totals, coef, picks, places
):
    half = weights[0].shape[1]
    groups = len(parts[0])
    total = groups * rows
    slots = groups * picks.shape[1] // 2
    outs = pl.pallas_call(
        functools.partial(finish_kernel, depth, block, last, parts, len(arrays)),
        out_shape=[jax.ShapeDtypeStruct((2, slots, half), jnp.bfloat16)]
        + [jax.ShapeDtypeStruct((rows, width), jnp.bfloat16)] * groups,
        in_specs=[SMEM] + [ANY] * len(arrays) + [HBM] * 6 + [VMEM] * 7,
        out_specs=[VMEM] * (1 + groups),
        scratch_shapes=[
            pltpu.VMEM((total, width), jnp.bfloat16),
            pltpu.VMEM((2, slots, width), jnp.bfloat16),
            pltpu.VMEM((4, width, half), jnp.bfloat16),
            pltpu.VMEM((2, half, width), jnp.bfloat16),
            pltpu.SemaphoreType.DMA((1, groups)),
            pltpu.SemaphoreType.DMA((4, 1)),
            pltpu.SemaphoreType.DMA((2,)),
        ],
        compiler_params=limit(28),
        cost_estimate=pl.CostEstimate(
            flops=12 * total * width * half,
            bytes_accessed=12 * width * half + 16 * total * half,
            transcendentals=2 * total * half,
        ),
    )(place, *arrays, *weights, *downs, *totals, coef, picks, places)
    return outs[0], outs[1:]


def descend_kernel(depth, blocks, groups, place_ref, hidden_ref, own_ref, other_ref, *refs):
    places_ref, refs = refs[0], refs[1:]
    y_refs, (d_all, sems) = refs[: groups * len(blocks)], refs[groups * len(blocks) :]
    width = d_all.shape[3]
    place = place_ref[0]
    copies = []
    for i, block in enumerate(blocks):
        target = lax.rem(place + block, depth)
        copies.append(
            [
                pltpu.make_async_copy(
                    ref.at[:, pl.ds(pl.multiple_of(target * width, width), width)],
                    d_all.at[i, k],
                    sems.at[i, k],
                )
                for k, ref in enumerate((own_ref, other_ref))
            ]
        )
    for pair in copies:
        for copy in pair:
            copy.start()
    for i, pair in enumerate(copies):
        for copy in pair:
            copy.wait()

        def put(group, y):
            y_refs[i * groups + group][...] = y

        spread(hidden_ref, d_all.at[i], places_ref, groups, put)


def descend(depth, place, blocks, groups, hidden, own, other, places):
    rows = places.shape[1]
    total = groups * rows
    half = own.shape[0]
    width = own.shape[1] // depth
    outs = pl.pallas_call(
        functools.partial(descend_kernel, depth, blocks, groups),
        out_shape=[jax.ShapeDtypeStruct((rows, width), jnp.bfloat16)] * (groups * len(blocks)),
        in_specs=[SMEM, VMEM, HBM, HBM, VMEM],
        out_specs=[VMEM] * (groups * len(blocks)),
        scratch_shapes=[
            pltpu.VMEM((len(blocks), 2, half, width), jnp.bfloat16),
            pltpu.SemaphoreType.DMA((len(blocks), 2)),
        ],
        compiler_params=limit(20),
        cost_estimate=pl.CostEstimate(
            flops=4 * total * len(blocks) * width * half,
            bytes_accessed=4 * len(blocks) * width * half + 2 * total * len(blocks) * width,
            transcendentals=0,
        ),
    )(place, hidden, own, other, places)
    return [outs[i * groups : (i + 1) * groups] for i in range(len(blocks))]


def after(value, *earlier):
    return lax.optimization_barrier((value,) + earlier)[0]


def fixed(value):
    return pltpu.with_memory_space_constraint(value, pltpu.HBM)


class Window:
    def __init__(self, size):
        self.size = size
        self.done = []

    def __call__(self, move, value, *earlier):
        if len(self.done) >= self.size:
            earlier += (self.done[-self.size],)
        self.done.append(move(after(value, *earlier) if earlier else value))
        return self.done[-1]


def gather_plan(tokens, routes, route_gates, gate_weight, up_weight, down_weight):
    devices = lax.axis_size("expert")
    depth = lax.axis_size("tensor")
    me = lax.axis_index("expert")
    spot = lax.axis_index("tensor").astype(jnp.int32)
    place = spot.reshape(1)
    wide, narrow = jnp.float32, jnp.bfloat16
    rows, width = tokens.shape

    def over(value, which):
        pairs = [(i, i ^ (2 if i % 2 == which else 4)) for i in range(devices)]
        return lax.ppermute(value, "expert", pairs)

    def near(value):
        return over(value, 0)

    def far(value):
        return over(value, 1)

    def twin(value):
        return lax.ppermute(value, "expert", [(i, i ^ 1) for i in range(devices)])

    def shift(by):
        pairs = [(i, (i + by) % depth) for i in range(depth)]
        return lambda value: lax.ppermute(value, "tensor", pairs)

    named = routes[:, :, None] == jnp.arange(devices, dtype=jnp.int32)[None, None, :]
    gates = jnp.sum(jnp.where(named, route_gates[:, :, None], 0.0), axis=1)
    high = gates.astype(narrow)
    rest = gates - high.astype(wide)
    middle = rest.astype(narrow)
    low = (rest - middle.astype(wide)).astype(narrow)
    extra = jnp.concatenate(
        [high, middle, low, jnp.zeros((rows, 128 - 3 * devices), narrow)], axis=1
    )
    marked = jnp.concatenate([tokens, extra], axis=1)

    plane, line = Window(3), Window(2)
    mine = [gate_weight[0], up_weight[0], down_weight[0]]
    other = [twin(w) for w in mine]
    z1 = shift(1)(tokens)
    b0 = far(marked)
    g0 = near(b0)
    a0 = near(after(marked, g0))
    z3 = shift(3)(after(tokens, g0))
    z13 = after(jnp.concatenate([z1, z3], axis=0), a0, *other)
    b13 = far(z13)
    a13 = near(z13)
    z2 = shift(1)(after(z1, a0, *other))
    g1 = shift(1)(after(g0, a0, *other))
    g3 = shift(3)(after(g0, a0, *other))
    b2 = far(z2)
    a2 = near(z2)
    weights = [fixed(w) for w in (mine[0], mine[1], other[0], other[1])]
    downs = [fixed(mine[2]), fixed(other[2])]
    def gates_of(value):
        parts = value[:, width : width + 3 * devices].astype(wide).reshape(rows, 3, devices)
        whole = jnp.sum(parts, axis=1)
        return jnp.concatenate(
            [
                lax.dynamic_slice_in_dim(whole, me, 1, axis=1),
                lax.dynamic_slice_in_dim(whole, me ^ 1, 1, axis=1),
            ],
            axis=1,
        )

    coef = jnp.stack([gates_of(v).T for v in (marked, a0, b0, g0)])
    routed = coef > 0.0
    earlier = jnp.arange(rows)[:, None] < jnp.arange(rows)[None, :]
    slot = jnp.dot(
        routed.reshape(-1, rows).astype(narrow),
        earlier.astype(narrow),
        preferred_element_type=wide,
    ).reshape(coef.shape)
    capacity = 2 * rows * routes.shape[1] // devices
    numbers = jnp.arange(capacity, dtype=jnp.int32).astype(wide)
    matches = (slot[:, :, None, :] == numbers[None, None, :, None]) & routed[:, :, None, :]
    picks = matches.reshape(4, 2 * capacity, rows).astype(narrow)
    places = jnp.swapaxes(picks, 1, 2)
    coef = jnp.sum(jnp.where(matches, coef[:, :, None, :], 0.0), axis=3)
    coef = jnp.swapaxes(coef, 1, 2).reshape(4 * capacity, 2)

    arrays = [marked, a0, b0, g0, z13, a13, b13, g1, g3]
    parts = [
        [(4, 0), (5, 0), (6, 0), (7, 0)],
        [(4, rows), (5, rows), (6, rows), (8, 0)],
        [(0, 0), (1, 0), (2, 0), (3, 0)],
    ]
    totals = project(
        depth, place, [1, 3, 0], arrays, parts, rows, width, weights, picks
    )
    g2 = near(b2)

    hidden, y2 = finish(
        depth, place, 2, 2, [z2, a2, b2, g2], [[(i, 0) for i in range(4)]], rows, width,
        weights, downs, totals, coef, picks, places,
    )
    y = {2: y2}
    late = [1, 3, 0]
    for d, part in zip(late, descend(depth, place, late, 4, hidden, *downs, places)):
        y[d] = part

    def plus(*values):
        total = values[0].astype(wide)
        for value in values[1:]:
            total = total + value.astype(wide)
        return total

    plane, line = Window(3), Window(2)
    pg2 = near(y[2][3])
    pa2 = near(y[2][1])
    zg1 = shift(1)(y[1][3])
    zg3 = shift(3)(y[3][3])
    pb2 = far(plus(y[2][2], pg2).astype(narrow))
    pa1 = near(y[1][1])
    pb1 = far(y[1][2])
    u2 = shift(1)(plus(y[2][0], pa2, pb2).astype(narrow))
    pa3 = near(after(y[3][1], pa2))
    pb3 = far(after(y[3][2], pb2))
    pg0 = near(plus(y[0][3], zg1, zg3).astype(narrow))
    pa0 = near(after(y[0][1], pg0))
    pb0 = far(plus(y[0][2], pg0).astype(narrow))
    t1 = shift(1)(plus(y[1][0], pa1, pb1, u2).astype(narrow))
    t3 = shift(3)(plus(y[3][0], pa3, pb3).astype(narrow))
    return plus(y[0][0], pa0, pb0, t1, t3).astype(narrow)


def solution(mesh):
    small = mesh.shape["expert"] == 8 and mesh.shape["tensor"] == 4
    return jax.shard_map(
        gather_plan if small else dispatch_plan,
        mesh=mesh,
        in_specs=(
            P("expert", "tensor"),
            P("expert", None),
            P("expert", None),
            P("expert", None, "tensor"),
            P("expert", None, "tensor"),
            P("expert", "tensor", None),
        ),
        out_specs=P("expert", "tensor"),
        check_vma=False,
    )
```

```python
import functools

import jax
import jax.numpy as jnp
from jax import lax
from jax.experimental import pallas as pl
from jax.experimental.pallas import tpu as pltpu
from jax.sharding import PartitionSpec as P

VMEM_BYTES = 40 * 1024 * 1024


def dispatch_plan(tokens, routes, route_gates, gate_weight, up_weight, down_weight):
    token_count = tokens.shape[0]
    slice_width = tokens.shape[1]
    route_count = routes.shape[1]
    source_count = lax.axis_size("expert")
    expert_count = gate_weight.shape[0] * source_count
    capacity = 2 * token_count * route_count // expert_count
    slot_total = source_count * capacity
    flat_routes = routes.reshape(-1)
    onehot = (flat_routes[:, None] == jnp.arange(expert_count, dtype=jnp.int32)[None, :]).astype(
        jnp.int32
    )
    before = jnp.cumsum(onehot, axis=0) - onehot
    slot_ids = jnp.sum(before * onehot, axis=1)
    places = flat_routes * capacity + slot_ids
    token_ids = jnp.arange(token_count * route_count, dtype=jnp.int32) // route_count
    outgoing = (
        jnp.zeros((expert_count * capacity, slice_width), jnp.bfloat16)
        .at[places]
        .set(tokens[token_ids])
    )
    outgoing = outgoing.reshape(expert_count, capacity, slice_width)
    arrived = lax.all_to_all(outgoing, "expert", split_axis=0, concat_axis=0, tiled=True)
    received = arrived.reshape(slot_total, slice_width)
    segment = lax.all_gather(received, "tensor", axis=1, tiled=True)
    gate_proj = jnp.dot(segment, gate_weight[0], preferred_element_type=jnp.float32)
    up_proj = jnp.dot(segment, up_weight[0], preferred_element_type=jnp.float32)
    hidden = (jax.nn.silu(gate_proj) * up_proj).astype(jnp.bfloat16)
    partial_value = lax.dot_general(
        down_weight[0], hidden, (((0,), (1,)), ((), ())), preferred_element_type=jnp.float32
    )
    summed = lax.psum_scatter(
        partial_value.astype(jnp.bfloat16), "tensor", scatter_dimension=0, tiled=True
    )
    expert_out = summed.reshape(slice_width, source_count, capacity)
    returned = lax.all_to_all(expert_out, "expert", split_axis=1, concat_axis=1, tiled=True)
    flat_back = returned.reshape(slice_width, expert_count * capacity)
    picked = jnp.take(flat_back, places, axis=1).astype(jnp.float32)
    weighted = picked * route_gates.reshape(-1)[None, :]
    combined = jnp.sum(weighted.reshape(slice_width, token_count, route_count), axis=2)
    return combined.T.astype(jnp.bfloat16)


ANY = pl.BlockSpec(memory_space=pl.ANY)
HBM = pl.BlockSpec(memory_space=pltpu.HBM)
VMEM = pl.BlockSpec(memory_space=pltpu.VMEM)
SMEM = pl.BlockSpec(memory_space=pltpu.SMEM)


def limit(size):
    return pltpu.CompilerParams(vmem_limit_bytes=size * 1024 * 1024)


def x_copies(parts, x_refs, x_all, sems, width):
    copies = []
    for i, block in enumerate(parts):
        for group, (number, first) in enumerate(block):
            rows = x_all.shape[0] // len(block)
            copies.append(
                pltpu.make_async_copy(
                    x_refs[number].at[pl.ds(first, rows), pl.ds(0, width)],
                    x_all.at[pl.ds(group * rows, rows), pl.ds(i * width, width)],
                    sems.at[i, group],
                )
            )
    return copies


def w_copies(blocks, depth, place, refs, w_all, sems, width):
    copies = [[] for _ in range(4)]
    for i, block in enumerate(blocks):
        source = lax.rem(place - block + depth, depth)
        rows = pl.ds(pl.multiple_of(source * width, width), width)
        for k in range(4):
            origin = refs[k].at[rows, :]
            copies[k].append(
                pltpu.make_async_copy(
                    origin, w_all.at[k, pl.ds(i * width, width), :], sems.at[k, i]
                )
            )
    return copies


def pick(x_all, picks_ref, xc_all, groups, columns):
    rows = x_all.shape[0] // groups
    slots = picks_ref.shape[1] // 2
    for group in range(groups):
        x = x_all[pl.ds(group * rows, rows), columns]
        z = jnp.dot(picks_ref[group], x, preferred_element_type=jnp.float32)
        z = z.astype(jnp.bfloat16)
        for expert in range(2):
            xc_all[expert, pl.ds(group * slots, slots), columns] = z[
                expert * slots : (expert + 1) * slots
            ]


def project_kernel(depth, blocks, parts, arrays, place_ref, *refs):
    x_refs, refs = refs[:arrays], refs[arrays:]
    w_refs, picks_ref, refs = refs[:4], refs[4], refs[5:]
    totals_refs, (x_all, xc_all, w_all, x_sems, w_sems) = refs[:4], refs[4:]
    groups = len(parts[0])
    width = x_all.shape[1] // len(blocks)
    xs = x_copies(parts, x_refs, x_all, x_sems, width)
    ws = w_copies(blocks, depth, place_ref[0], w_refs, w_all, w_sems, width)
    for copy in xs + ws[0] + ws[1] + ws[2] + ws[3]:
        copy.start()
    for i in range(len(blocks)):
        for copy in xs[i * groups : (i + 1) * groups]:
            copy.wait()
        pick(x_all, picks_ref, xc_all, groups, pl.ds(i * width, width))
    for k in range(4):
        for copy in ws[k]:
            copy.wait()
        totals_refs[k][...] = jnp.dot(
            xc_all[k // 2], w_all[k], preferred_element_type=jnp.float32
        )


def project(depth, place, blocks, arrays, parts, rows, width, weights, picks):
    half = weights[0].shape[1]
    groups = len(parts[0])
    total = rows * groups
    slots = groups * picks.shape[1] // 2
    span = len(blocks) * width
    return pl.pallas_call(
        functools.partial(project_kernel, depth, blocks, parts, len(arrays)),
        out_shape=[jax.ShapeDtypeStruct((slots, half), jnp.float32)] * 4,
        in_specs=[SMEM] + [ANY] * len(arrays) + [HBM] * 4 + [VMEM],
        out_specs=[VMEM] * 4,
        scratch_shapes=[
            pltpu.VMEM((total, span), jnp.bfloat16),
            pltpu.VMEM((2, slots, span), jnp.bfloat16),
            pltpu.VMEM((4, span, half), jnp.bfloat16),
            pltpu.SemaphoreType.DMA((len(blocks), groups)),
            pltpu.SemaphoreType.DMA((4, len(blocks))),
        ],
        compiler_params=limit(28),
        cost_estimate=pl.CostEstimate(
            flops=8 * total * span * half,
            bytes_accessed=8 * span * half + 16 * total * half,
            transcendentals=0,
        ),
    )(place, *arrays, *weights, picks)


def spread(hidden_ref, downs, places_ref, groups, put):
    slots = hidden_ref.shape[1] // groups
    each = [
        jnp.dot(hidden_ref[expert], downs[expert], preferred_element_type=jnp.float32).astype(
            jnp.bfloat16
        )
        for expert in range(2)
    ]
    for group in range(groups):
        part = slice(group * slots, (group + 1) * slots)
        both = jnp.concatenate([each[0][part], each[1][part]], axis=0)
        y = jnp.dot(places_ref[group], both, preferred_element_type=jnp.float32)
        put(group, y.astype(jnp.bfloat16))


def finish_kernel(depth, block, last, parts, arrays, place_ref, *refs):
    x_refs, refs = refs[:arrays], refs[arrays:]
    w_refs, down_refs, refs = refs[:4], refs[4:6], refs[6:]
    totals_refs, coef_ref, picks_ref, places_ref, refs = refs[:4], *refs[4:7], refs[7:]
    groups = len(parts[0])
    hidden_ref, y_refs, refs = refs[0], refs[1 : 1 + groups], refs[1 + groups :]
    x_all, xc_all, w_all, d_all, x_sems, w_sems, d_sems = refs
    width = x_all.shape[1]
    place = place_ref[0]
    xs = x_copies(parts, x_refs, x_all, x_sems, width)
    ws = w_copies([block], depth, place, w_refs, w_all, w_sems, width)
    target = lax.rem(place + last, depth)
    ds = [
        pltpu.make_async_copy(
            down_refs[k].at[:, pl.ds(pl.multiple_of(target * width, width), width)],
            d_all.at[k],
            d_sems.at[k],
        )
        for k in range(2)
    ]
    for copy in xs + ws[0] + ws[1] + ws[2] + ws[3] + ds:
        copy.start()
    for copy in xs:
        copy.wait()
    pick(x_all, picks_ref, xc_all, groups, pl.ds(0, width))
    for expert in range(2):
        for copy in ws[2 * expert] + ws[2 * expert + 1]:
            copy.wait()
        gate, up = [
            totals_refs[j][...]
            + jnp.dot(xc_all[expert], w_all[j], preferred_element_type=jnp.float32)
            for j in (2 * expert, 2 * expert + 1)
        ]
        value = gate / (1.0 + jnp.exp(-gate)) * up * coef_ref[:, expert : expert + 1]
        hidden_ref[expert] = value.astype(jnp.bfloat16)
    for copy in ds:
        copy.wait()

    def put(group, y):
        y_refs[group][...] = y

    spread(hidden_ref, d_all, places_ref, groups, put)


def finish(
    depth, place, block, last, arrays, parts, rows, width, weights, downs, totals, coef, picks, places
):
    half = weights[0].shape[1]
    groups = len(parts[0])
    total = groups * rows
    slots = groups * picks.shape[1] // 2
    outs = pl.pallas_call(
        functools.partial(finish_kernel, depth, block, last, parts, len(arrays)),
        out_shape=[jax.ShapeDtypeStruct((2, slots, half), jnp.bfloat16)]
        + [jax.ShapeDtypeStruct((rows, width), jnp.bfloat16)] * groups,
        in_specs=[SMEM] + [ANY] * len(arrays) + [HBM] * 6 + [VMEM] * 7,
        out_specs=[VMEM] * (1 + groups),
        scratch_shapes=[
            pltpu.VMEM((total, width), jnp.bfloat16),
            pltpu.VMEM((2, slots, width), jnp.bfloat16),
            pltpu.VMEM((4, width, half), jnp.bfloat16),
            pltpu.VMEM((2, half, width), jnp.bfloat16),
            pltpu.SemaphoreType.DMA((1, groups)),
            pltpu.SemaphoreType.DMA((4, 1)),
            pltpu.SemaphoreType.DMA((2,)),
        ],
        compiler_params=limit(28),
        cost_estimate=pl.CostEstimate(
            flops=12 * total * width * half,
            bytes_accessed=12 * width * half + 16 * total * half,
            transcendentals=2 * total * half,
        ),
    )(place, *arrays, *weights, *downs, *totals, coef, picks, places)
    return outs[0], outs[1:]


def descend_kernel(depth, blocks, groups, place_ref, hidden_ref, own_ref, other_ref, *refs):
    places_ref, refs = refs[0], refs[1:]
    y_refs, (d_all, sems) = refs[: groups * len(blocks)], refs[groups * len(blocks) :]
    width = d_all.shape[3]
    place = place_ref[0]
    copies = []
    for i, block in enumerate(blocks):
        target = lax.rem(place + block, depth)
        copies.append(
            [
                pltpu.make_async_copy(
                    ref.at[:, pl.ds(pl.multiple_of(target * width, width), width)],
                    d_all.at[i, k],
                    sems.at[i, k],
                )
                for k, ref in enumerate((own_ref, other_ref))
            ]
        )
    for pair in copies:
        for copy in pair:
            copy.start()
    for i, pair in enumerate(copies):
        for copy in pair:
            copy.wait()

        def put(group, y):
            y_refs[i * groups + group][...] = y

        spread(hidden_ref, d_all.at[i], places_ref, groups, put)


def descend(depth, place, blocks, groups, hidden, own, other, places):
    rows = places.shape[1]
    total = groups * rows
    half = own.shape[0]
    width = own.shape[1] // depth
    outs = pl.pallas_call(
        functools.partial(descend_kernel, depth, blocks, groups),
        out_shape=[jax.ShapeDtypeStruct((rows, width), jnp.bfloat16)] * (groups * len(blocks)),
        in_specs=[SMEM, VMEM, HBM, HBM, VMEM],
        out_specs=[VMEM] * (groups * len(blocks)),
        scratch_shapes=[
            pltpu.VMEM((len(blocks), 2, half, width), jnp.bfloat16),
            pltpu.SemaphoreType.DMA((len(blocks), 2)),
        ],
        compiler_params=limit(20),
        cost_estimate=pl.CostEstimate(
            flops=4 * total * len(blocks) * width * half,
            bytes_accessed=4 * len(blocks) * width * half + 2 * total * len(blocks) * width,
            transcendentals=0,
        ),
    )(place, hidden, own, other, places)
    return [outs[i * groups : (i + 1) * groups] for i in range(len(blocks))]


def after(value, *earlier):
    return lax.optimization_barrier((value,) + earlier)[0]


def fixed(value):
    return pltpu.with_memory_space_constraint(value, pltpu.HBM)


class Window:
    def __init__(self, size):
        self.size = size
        self.done = []

    def __call__(self, move, value, *earlier):
        if len(self.done) >= self.size:
            earlier += (self.done[-self.size],)
        self.done.append(move(after(value, *earlier) if earlier else value))
        return self.done[-1]


def gather_plan(tokens, routes, route_gates, gate_weight, up_weight, down_weight):
    devices = lax.axis_size("expert")
    depth = lax.axis_size("tensor")
    me = lax.axis_index("expert")
    spot = lax.axis_index("tensor").astype(jnp.int32)
    place = spot.reshape(1)
    wide, narrow = jnp.float32, jnp.bfloat16
    rows, width = tokens.shape

    def over(value, which):
        pairs = [(i, i ^ (2 if i % 2 == which else 4)) for i in range(devices)]
        return lax.ppermute(value, "expert", pairs)

    def near(value):
        return over(value, 0)

    def far(value):
        return over(value, 1)

    def twin(value):
        return lax.ppermute(value, "expert", [(i, i ^ 1) for i in range(devices)])

    def shift(by):
        pairs = [(i, (i + by) % depth) for i in range(depth)]
        return lambda value: lax.ppermute(value, "tensor", pairs)

    named = routes[:, :, None] == jnp.arange(devices, dtype=jnp.int32)[None, None, :]
    gates = jnp.sum(jnp.where(named, route_gates[:, :, None], 0.0), axis=1)
    high = gates.astype(narrow)
    rest = gates - high.astype(wide)
    middle = rest.astype(narrow)
    low = (rest - middle.astype(wide)).astype(narrow)
    extra = jnp.concatenate(
        [high, middle, low, jnp.zeros((rows, 128 - 3 * devices), narrow)], axis=1
    )
    marked = jnp.concatenate([tokens, extra], axis=1)

    plane, line = Window(3), Window(2)
    mine = [gate_weight[0], up_weight[0], down_weight[0]]
    other = [twin(w) for w in mine]
    z1 = shift(1)(tokens)
    b0 = far(marked)
    g0 = near(b0)
    a0 = near(after(marked, g0))
    z3 = shift(3)(after(tokens, g0))
    z13 = after(jnp.concatenate([z1, z3], axis=0), a0, *other)
    b13 = far(z13)
    a13 = near(z13)
    z2 = shift(1)(after(z1, a0, *other))
    g1 = shift(1)(after(g0, z2))
    g3 = near(b13[rows:])
    b2 = far(z2)
    a2 = near(z2)
    weights = [fixed(w) for w in (mine[0], mine[1], other[0], other[1])]
    downs = [fixed(mine[2]), fixed(other[2])]
    def gates_of(value):
        parts = value[:, width : width + 3 * devices].astype(wide).reshape(rows, 3, devices)
        whole = jnp.sum(parts, axis=1)
        return jnp.concatenate(
            [
                lax.dynamic_slice_in_dim(whole, me, 1, axis=1),
                lax.dynamic_slice_in_dim(whole, me ^ 1, 1, axis=1),
            ],
            axis=1,
        )

    coef = jnp.stack([gates_of(v).T for v in (marked, a0, b0, g0)])
    routed = coef > 0.0
    earlier = jnp.arange(rows)[:, None] < jnp.arange(rows)[None, :]
    slot = jnp.dot(
        routed.reshape(-1, rows).astype(narrow),
        earlier.astype(narrow),
        preferred_element_type=wide,
    ).reshape(coef.shape)
    capacity = 2 * rows * routes.shape[1] // devices
    numbers = jnp.arange(capacity, dtype=jnp.int32).astype(wide)
    matches = (slot[:, :, None, :] == numbers[None, None, :, None]) & routed[:, :, None, :]
    picks = matches.reshape(4, 2 * capacity, rows).astype(narrow)
    places = jnp.swapaxes(picks, 1, 2)
    coef = jnp.sum(jnp.where(matches, coef[:, :, None, :], 0.0), axis=3)
    coef = jnp.swapaxes(coef, 1, 2).reshape(4 * capacity, 2)

    arrays = [marked, a0, b0, g0, z13, a13, b13, g1, g3]
    parts = [
        [(4, 0), (5, 0), (6, 0), (7, 0)],
        [(4, rows), (5, rows), (6, rows), (8, 0)],
        [(0, 0), (1, 0), (2, 0), (3, 0)],
    ]
    totals = project(
        depth, place, [1, 3, 0], arrays, parts, rows, width, weights, picks
    )
    g2 = near(b2)

    hidden, y2 = finish(
        depth, place, 2, 2, [z2, a2, b2, g2], [[(i, 0) for i in range(4)]], rows, width,
        weights, downs, totals, coef, picks, places,
    )
    y = {2: y2}
    late = [1, 3, 0]
    for d, part in zip(late, descend(depth, place, late, 4, hidden, *downs, places)):
        y[d] = part

    def plus(*values):
        total = values[0].astype(wide)
        for value in values[1:]:
            total = total + value.astype(wide)
        return total

    plane, line = Window(3), Window(2)
    pg2 = near(y[2][3])
    pa2 = near(y[2][1])
    zg1 = shift(1)(y[1][3])
    zg3 = shift(3)(y[3][3])
    pb2 = far(plus(y[2][2], pg2).astype(narrow))
    pa1 = near(y[1][1])
    pb1 = far(y[1][2])
    u2 = shift(1)(plus(y[2][0], pa2, pb2).astype(narrow))
    pa3 = near(after(y[3][1], pa2))
    pb3 = far(after(y[3][2], pb2))
    pg0 = near(plus(y[0][3], zg1, zg3).astype(narrow))
    pa0 = near(after(y[0][1], pg0))
    pb0 = far(plus(y[0][2], pg0).astype(narrow))
    t1 = shift(1)(plus(y[1][0], pa1, pb1, u2).astype(narrow))
    t3 = shift(3)(plus(y[3][0], pa3, pb3).astype(narrow))
    return plus(y[0][0], pa0, pb0, t1, t3).astype(narrow)


def solution(mesh):
    small = mesh.shape["expert"] == 8 and mesh.shape["tensor"] == 4
    return jax.shard_map(
        gather_plan if small else dispatch_plan,
        mesh=mesh,
        in_specs=(
            P("expert", "tensor"),
            P("expert", None),
            P("expert", None),
            P("expert", None, "tensor"),
            P("expert", None, "tensor"),
            P("expert", "tensor", None),
        ),
        out_specs=P("expert", "tensor"),
        check_vma=False,
    )
```

```python
import functools

import jax
import jax.numpy as jnp
from jax import lax
from jax.experimental import pallas as pl
from jax.experimental.pallas import tpu as pltpu
from jax.sharding import PartitionSpec as P

VMEM_BYTES = 40 * 1024 * 1024


def dispatch_plan(tokens, routes, route_gates, gate_weight, up_weight, down_weight):
    token_count = tokens.shape[0]
    slice_width = tokens.shape[1]
    route_count = routes.shape[1]
    source_count = lax.axis_size("expert")
    expert_count = gate_weight.shape[0] * source_count
    capacity = 2 * token_count * route_count // expert_count
    slot_total = source_count * capacity
    flat_routes = routes.reshape(-1)
    onehot = (flat_routes[:, None] == jnp.arange(expert_count, dtype=jnp.int32)[None, :]).astype(
        jnp.int32
    )
    before = jnp.cumsum(onehot, axis=0) - onehot
    slot_ids = jnp.sum(before * onehot, axis=1)
    places = flat_routes * capacity + slot_ids
    token_ids = jnp.arange(token_count * route_count, dtype=jnp.int32) // route_count
    outgoing = (
        jnp.zeros((expert_count * capacity, slice_width), jnp.bfloat16)
        .at[places]
        .set(tokens[token_ids])
    )
    outgoing = outgoing.reshape(expert_count, capacity, slice_width)
    arrived = lax.all_to_all(outgoing, "expert", split_axis=0, concat_axis=0, tiled=True)
    received = arrived.reshape(slot_total, slice_width)
    segment = lax.all_gather(received, "tensor", axis=1, tiled=True)
    gate_proj = jnp.dot(segment, gate_weight[0], preferred_element_type=jnp.float32)
    up_proj = jnp.dot(segment, up_weight[0], preferred_element_type=jnp.float32)
    hidden = (jax.nn.silu(gate_proj) * up_proj).astype(jnp.bfloat16)
    partial_value = lax.dot_general(
        down_weight[0], hidden, (((0,), (1,)), ((), ())), preferred_element_type=jnp.float32
    )
    summed = lax.psum_scatter(
        partial_value.astype(jnp.bfloat16), "tensor", scatter_dimension=0, tiled=True
    )
    expert_out = summed.reshape(slice_width, source_count, capacity)
    returned = lax.all_to_all(expert_out, "expert", split_axis=1, concat_axis=1, tiled=True)
    flat_back = returned.reshape(slice_width, expert_count * capacity)
    picked = jnp.take(flat_back, places, axis=1).astype(jnp.float32)
    weighted = picked * route_gates.reshape(-1)[None, :]
    combined = jnp.sum(weighted.reshape(slice_width, token_count, route_count), axis=2)
    return combined.T.astype(jnp.bfloat16)


ANY = pl.BlockSpec(memory_space=pl.ANY)
HBM = pl.BlockSpec(memory_space=pltpu.HBM)
VMEM = pl.BlockSpec(memory_space=pltpu.VMEM)
SMEM = pl.BlockSpec(memory_space=pltpu.SMEM)


def limit(size):
    return pltpu.CompilerParams(vmem_limit_bytes=size * 1024 * 1024)


def x_copies(parts, x_refs, x_all, sems, width):
    copies = []
    for i, block in enumerate(parts):
        for group, (number, first) in enumerate(block):
            rows = x_all.shape[0] // len(block)
            copies.append(
                pltpu.make_async_copy(
                    x_refs[number].at[pl.ds(first, rows), pl.ds(0, width)],
                    x_all.at[pl.ds(group * rows, rows), pl.ds(i * width, width)],
                    sems.at[i, group],
                )
            )
    return copies


def w_copies(blocks, depth, place, refs, w_all, sems, width):
    copies = [[] for _ in range(4)]
    for i, block in enumerate(blocks):
        source = lax.rem(place - block + depth, depth)
        rows = pl.ds(pl.multiple_of(source * width, width), width)
        for k in range(4):
            origin = refs[k].at[rows, :]
            copies[k].append(
                pltpu.make_async_copy(
                    origin, w_all.at[k, pl.ds(i * width, width), :], sems.at[k, i]
                )
            )
    return copies


def pick(x_all, picks_ref, xc_all, groups, columns):
    rows = x_all.shape[0] // groups
    slots = picks_ref.shape[1] // 2
    for group in range(groups):
        x = x_all[pl.ds(group * rows, rows), columns]
        z = jnp.dot(picks_ref[group], x, preferred_element_type=jnp.float32)
        z = z.astype(jnp.bfloat16)
        for expert in range(2):
            xc_all[expert, pl.ds(group * slots, slots), columns] = z[
                expert * slots : (expert + 1) * slots
            ]


def project_kernel(depth, blocks, parts, arrays, place_ref, *refs):
    x_refs, refs = refs[:arrays], refs[arrays:]
    w_refs, picks_ref, refs = refs[:4], refs[4], refs[5:]
    totals_refs, (x_all, xc_all, w_all, x_sems, w_sems) = refs[:4], refs[4:]
    groups = len(parts[0])
    width = x_all.shape[1] // len(blocks)
    xs = x_copies(parts, x_refs, x_all, x_sems, width)
    ws = w_copies(blocks, depth, place_ref[0], w_refs, w_all, w_sems, width)
    for copy in xs + ws[0] + ws[1] + ws[2] + ws[3]:
        copy.start()
    for i in range(len(blocks)):
        for copy in xs[i * groups : (i + 1) * groups]:
            copy.wait()
        pick(x_all, picks_ref, xc_all, groups, pl.ds(i * width, width))
    for k in range(4):
        for copy in ws[k]:
            copy.wait()
        totals_refs[k][...] = jnp.dot(
            xc_all[k // 2], w_all[k], preferred_element_type=jnp.float32
        )


def project(depth, place, blocks, arrays, parts, rows, width, weights, picks):
    half = weights[0].shape[1]
    groups = len(parts[0])
    total = rows * groups
    slots = groups * picks.shape[1] // 2
    span = len(blocks) * width
    return pl.pallas_call(
        functools.partial(project_kernel, depth, blocks, parts, len(arrays)),
        out_shape=[jax.ShapeDtypeStruct((slots, half), jnp.float32)] * 4,
        in_specs=[SMEM] + [ANY] * len(arrays) + [HBM] * 4 + [VMEM],
        out_specs=[VMEM] * 4,
        scratch_shapes=[
            pltpu.VMEM((total, span), jnp.bfloat16),
            pltpu.VMEM((2, slots, span), jnp.bfloat16),
            pltpu.VMEM((4, span, half), jnp.bfloat16),
            pltpu.SemaphoreType.DMA((len(blocks), groups)),
            pltpu.SemaphoreType.DMA((4, len(blocks))),
        ],
        compiler_params=limit(28),
        cost_estimate=pl.CostEstimate(
            flops=8 * total * span * half,
            bytes_accessed=8 * span * half + 16 * total * half,
            transcendentals=0,
        ),
    )(place, *arrays, *weights, picks)


def spread(hidden_ref, downs, places_ref, groups, put):
    slots = hidden_ref.shape[1] // groups
    each = [
        jnp.dot(hidden_ref[expert], downs[expert], preferred_element_type=jnp.float32).astype(
            jnp.bfloat16
        )
        for expert in range(2)
    ]
    for group in range(groups):
        part = slice(group * slots, (group + 1) * slots)
        both = jnp.concatenate([each[0][part], each[1][part]], axis=0)
        y = jnp.dot(places_ref[group], both, preferred_element_type=jnp.float32)
        put(group, y.astype(jnp.bfloat16))


def finish_kernel(depth, block, last, parts, arrays, place_ref, *refs):
    x_refs, refs = refs[:arrays], refs[arrays:]
    w_refs, down_refs, refs = refs[:4], refs[4:6], refs[6:]
    totals_refs, coef_ref, picks_ref, places_ref, refs = refs[:4], *refs[4:7], refs[7:]
    groups = len(parts[0])
    hidden_ref, y_refs, refs = refs[0], refs[1 : 1 + groups], refs[1 + groups :]
    x_all, xc_all, w_all, d_all, x_sems, w_sems, d_sems = refs
    width = x_all.shape[1]
    place = place_ref[0]
    xs = x_copies(parts, x_refs, x_all, x_sems, width)
    ws = w_copies([block], depth, place, w_refs, w_all, w_sems, width)
    target = lax.rem(place + last, depth)
    ds = [
        pltpu.make_async_copy(
            down_refs[k].at[:, pl.ds(pl.multiple_of(target * width, width), width)],
            d_all.at[k],
            d_sems.at[k],
        )
        for k in range(2)
    ]
    for copy in xs + ws[0] + ws[1] + ws[2] + ws[3] + ds:
        copy.start()
    for copy in xs:
        copy.wait()
    pick(x_all, picks_ref, xc_all, groups, pl.ds(0, width))
    for expert in range(2):
        for copy in ws[2 * expert] + ws[2 * expert + 1]:
            copy.wait()
        gate, up = [
            totals_refs[j][...]
            + jnp.dot(xc_all[expert], w_all[j], preferred_element_type=jnp.float32)
            for j in (2 * expert, 2 * expert + 1)
        ]
        value = gate / (1.0 + jnp.exp(-gate)) * up * coef_ref[:, expert : expert + 1]
        hidden_ref[expert] = value.astype(jnp.bfloat16)
    for copy in ds:
        copy.wait()

    def put(group, y):
        y_refs[group][...] = y

    spread(hidden_ref, d_all, places_ref, groups, put)


def finish(
    depth, place, block, last, arrays, parts, rows, width, weights, downs, totals, coef, picks, places
):
    half = weights[0].shape[1]
    groups = len(parts[0])
    total = groups * rows
    slots = groups * picks.shape[1] // 2
    outs = pl.pallas_call(
        functools.partial(finish_kernel, depth, block, last, parts, len(arrays)),
        out_shape=[jax.ShapeDtypeStruct((2, slots, half), jnp.bfloat16)]
        + [jax.ShapeDtypeStruct((rows, width), jnp.bfloat16)] * groups,
        in_specs=[SMEM] + [ANY] * len(arrays) + [HBM] * 6 + [VMEM] * 7,
        out_specs=[VMEM] * (1 + groups),
        scratch_shapes=[
            pltpu.VMEM((total, width), jnp.bfloat16),
            pltpu.VMEM((2, slots, width), jnp.bfloat16),
            pltpu.VMEM((4, width, half), jnp.bfloat16),
            pltpu.VMEM((2, half, width), jnp.bfloat16),
            pltpu.SemaphoreType.DMA((1, groups)),
            pltpu.SemaphoreType.DMA((4, 1)),
            pltpu.SemaphoreType.DMA((2,)),
        ],
        compiler_params=limit(28),
        cost_estimate=pl.CostEstimate(
            flops=12 * total * width * half,
            bytes_accessed=12 * width * half + 16 * total * half,
            transcendentals=2 * total * half,
        ),
    )(place, *arrays, *weights, *downs, *totals, coef, picks, places)
    return outs[0], outs[1:]


def descend_kernel(depth, blocks, groups, place_ref, hidden_ref, own_ref, other_ref, *refs):
    places_ref, refs = refs[0], refs[1:]
    y_refs, (d_all, sems) = refs[: groups * len(blocks)], refs[groups * len(blocks) :]
    width = d_all.shape[3]
    place = place_ref[0]
    copies = []
    for i, block in enumerate(blocks):
        target = lax.rem(place + block, depth)
        copies.append(
            [
                pltpu.make_async_copy(
                    ref.at[:, pl.ds(pl.multiple_of(target * width, width), width)],
                    d_all.at[i, k],
                    sems.at[i, k],
                )
                for k, ref in enumerate((own_ref, other_ref))
            ]
        )
    for pair in copies:
        for copy in pair:
            copy.start()
    for i, pair in enumerate(copies):
        for copy in pair:
            copy.wait()

        def put(group, y):
            y_refs[i * groups + group][...] = y

        spread(hidden_ref, d_all.at[i], places_ref, groups, put)


def descend(depth, place, blocks, groups, hidden, own, other, places):
    rows = places.shape[1]
    total = groups * rows
    half = own.shape[0]
    width = own.shape[1] // depth
    outs = pl.pallas_call(
        functools.partial(descend_kernel, depth, blocks, groups),
        out_shape=[jax.ShapeDtypeStruct((rows, width), jnp.bfloat16)] * (groups * len(blocks)),
        in_specs=[SMEM, VMEM, HBM, HBM, VMEM],
        out_specs=[VMEM] * (groups * len(blocks)),
        scratch_shapes=[
            pltpu.VMEM((len(blocks), 2, half, width), jnp.bfloat16),
            pltpu.SemaphoreType.DMA((len(blocks), 2)),
        ],
        compiler_params=limit(20),
        cost_estimate=pl.CostEstimate(
            flops=4 * total * len(blocks) * width * half,
            bytes_accessed=4 * len(blocks) * width * half + 2 * total * len(blocks) * width,
            transcendentals=0,
        ),
    )(place, hidden, own, other, places)
    return [outs[i * groups : (i + 1) * groups] for i in range(len(blocks))]


def after(value, *earlier):
    return lax.optimization_barrier((value,) + earlier)[0]


def fixed(value):
    return pltpu.with_memory_space_constraint(value, pltpu.HBM)


class Window:
    def __init__(self, size):
        self.size = size
        self.done = []

    def __call__(self, move, value, *earlier):
        if len(self.done) >= self.size:
            earlier += (self.done[-self.size],)
        self.done.append(move(after(value, *earlier) if earlier else value))
        return self.done[-1]


def gather_plan(tokens, routes, route_gates, gate_weight, up_weight, down_weight):
    devices = lax.axis_size("expert")
    depth = lax.axis_size("tensor")
    me = lax.axis_index("expert")
    spot = lax.axis_index("tensor").astype(jnp.int32)
    place = spot.reshape(1)
    wide, narrow = jnp.float32, jnp.bfloat16
    rows, width = tokens.shape

    def over(value, which):
        pairs = [(i, i ^ (2 if i % 2 == which else 4)) for i in range(devices)]
        return lax.ppermute(value, "expert", pairs)

    def near(value):
        return over(value, 0)

    def far(value):
        return over(value, 1)

    def twin(value):
        return lax.ppermute(value, "expert", [(i, i ^ 1) for i in range(devices)])

    def shift(by):
        pairs = [(i, (i + by) % depth) for i in range(depth)]
        return lambda value: lax.ppermute(value, "tensor", pairs)

    named = routes[:, :, None] == jnp.arange(devices, dtype=jnp.int32)[None, None, :]
    gates = jnp.sum(jnp.where(named, route_gates[:, :, None], 0.0), axis=1)
    high = gates.astype(narrow)
    rest = gates - high.astype(wide)
    middle = rest.astype(narrow)
    low = (rest - middle.astype(wide)).astype(narrow)
    extra = jnp.concatenate(
        [high, middle, low, jnp.zeros((rows, 128 - 3 * devices), narrow)], axis=1
    )
    marked = jnp.concatenate([tokens, extra], axis=1)

    plane, line = Window(3), Window(2)
    mine = [gate_weight[0], up_weight[0], down_weight[0]]
    other = [twin(w) for w in mine]
    z1 = shift(1)(tokens)
    b0 = far(marked)
    g0 = near(b0)
    a0 = near(after(marked, g0))
    z3 = shift(3)(after(tokens, g0))
    z13 = after(jnp.concatenate([z1, z3], axis=0), a0, *other)
    b13 = far(z13)
    a13 = near(z13)
    z2 = shift(1)(after(z1, a0, *other))
    g1 = shift(1)(after(g0, z2))
    g3 = near(b13[rows:])
    b2 = far(z2)
    a2 = near(z2)
    weights = [fixed(w) for w in (mine[0], mine[1], other[0], other[1])]
    downs = [fixed(mine[2]), fixed(other[2])]
    def gates_of(value):
        parts = value[:, width : width + 3 * devices].astype(wide).reshape(rows, 3, devices)
        whole = jnp.sum(parts, axis=1)
        return jnp.concatenate(
            [
                lax.dynamic_slice_in_dim(whole, me, 1, axis=1),
                lax.dynamic_slice_in_dim(whole, me ^ 1, 1, axis=1),
            ],
            axis=1,
        )

    coef = jnp.stack([gates_of(v).T for v in (marked, a0, b0, g0)])
    routed = coef > 0.0
    earlier = jnp.arange(rows)[:, None] < jnp.arange(rows)[None, :]
    slot = jnp.dot(
        routed.reshape(-1, rows).astype(narrow),
        earlier.astype(narrow),
        preferred_element_type=wide,
    ).reshape(coef.shape)
    capacity = 2 * rows * routes.shape[1] // devices
    numbers = jnp.arange(capacity, dtype=jnp.int32).astype(wide)
    matches = (slot[:, :, None, :] == numbers[None, None, :, None]) & routed[:, :, None, :]
    picks = matches.reshape(4, 2 * capacity, rows).astype(narrow)
    places = jnp.swapaxes(picks, 1, 2)
    coef = jnp.sum(jnp.where(matches, coef[:, :, None, :], 0.0), axis=3)
    coef = jnp.swapaxes(coef, 1, 2).reshape(4 * capacity, 2)

    arrays = [marked, a0, b0, g0, z13, a13, b13, g1, g3]
    parts = [
        [(4, 0), (5, 0), (6, 0), (7, 0)],
        [(4, rows), (5, rows), (6, rows), (8, 0)],
        [(0, 0), (1, 0), (2, 0), (3, 0)],
    ]
    totals = project(
        depth, place, [1, 3, 0], arrays, parts, rows, width, weights, picks
    )
    g2 = near(b2)

    hidden, y2 = finish(
        depth, place, 2, 2, [z2, a2, b2, g2], [[(i, 0) for i in range(4)]], rows, width,
        weights, downs, totals, coef, picks, places,
    )
    y = {2: y2}
    for late in ([1, 3], [0]):
        parts = descend(depth, place, late, 4, hidden, *downs, places)
        for d, part in zip(late, parts):
            y[d] = part

    def plus(*values):
        total = values[0].astype(wide)
        for value in values[1:]:
            total = total + value.astype(wide)
        return total

    plane, line = Window(3), Window(2)
    pg2 = near(y[2][3])
    pa2 = near(y[2][1])
    zg1 = shift(1)(y[1][3])
    zg3 = shift(3)(y[3][3])
    pb2 = far(plus(y[2][2], pg2).astype(narrow))
    pa1 = near(after(y[1][1], pa2))
    pb1 = far(after(y[1][2], pb2))
    u2 = shift(1)(plus(y[2][0], pa2, pb2).astype(narrow))
    pa3 = near(y[3][1])
    pb3 = far(y[3][2])
    pg0 = near(plus(y[0][3], zg1, zg3).astype(narrow))
    pa0 = near(after(y[0][1], pg0))
    pb0 = far(plus(y[0][2], pg0).astype(narrow))
    t1 = shift(1)(plus(y[1][0], pa1, pb1, u2).astype(narrow))
    t3 = shift(3)(plus(y[3][0], pa3, pb3).astype(narrow))
    return plus(y[0][0], pa0, pb0, t1, t3).astype(narrow)


def solution(mesh):
    small = mesh.shape["expert"] == 8 and mesh.shape["tensor"] == 4
    return jax.shard_map(
        gather_plan if small else dispatch_plan,
        mesh=mesh,
        in_specs=(
            P("expert", "tensor"),
            P("expert", None),
            P("expert", None),
            P("expert", None, "tensor"),
            P("expert", None, "tensor"),
            P("expert", "tensor", None),
        ),
        out_specs=P("expert", "tensor"),
        check_vma=False,
    )
```

```python
import functools

import jax
import jax.numpy as jnp
from jax import lax
from jax.experimental import pallas as pl
from jax.experimental.pallas import tpu as pltpu
from jax.sharding import PartitionSpec as P

VMEM_BYTES = 40 * 1024 * 1024


def dispatch_plan(tokens, routes, route_gates, gate_weight, up_weight, down_weight):
    token_count = tokens.shape[0]
    slice_width = tokens.shape[1]
    route_count = routes.shape[1]
    source_count = lax.axis_size("expert")
    expert_count = gate_weight.shape[0] * source_count
    capacity = 2 * token_count * route_count // expert_count
    slot_total = source_count * capacity
    flat_routes = routes.reshape(-1)
    onehot = (flat_routes[:, None] == jnp.arange(expert_count, dtype=jnp.int32)[None, :]).astype(
        jnp.int32
    )
    before = jnp.cumsum(onehot, axis=0) - onehot
    slot_ids = jnp.sum(before * onehot, axis=1)
    places = flat_routes * capacity + slot_ids
    token_ids = jnp.arange(token_count * route_count, dtype=jnp.int32) // route_count
    outgoing = (
        jnp.zeros((expert_count * capacity, slice_width), jnp.bfloat16)
        .at[places]
        .set(tokens[token_ids])
    )
    outgoing = outgoing.reshape(expert_count, capacity, slice_width)
    arrived = lax.all_to_all(outgoing, "expert", split_axis=0, concat_axis=0, tiled=True)
    received = arrived.reshape(slot_total, slice_width)
    segment = lax.all_gather(received, "tensor", axis=1, tiled=True)
    gate_proj = jnp.dot(segment, gate_weight[0], preferred_element_type=jnp.float32)
    up_proj = jnp.dot(segment, up_weight[0], preferred_element_type=jnp.float32)
    hidden = (jax.nn.silu(gate_proj) * up_proj).astype(jnp.bfloat16)
    partial_value = lax.dot_general(
        down_weight[0], hidden, (((0,), (1,)), ((), ())), preferred_element_type=jnp.float32
    )
    summed = lax.psum_scatter(
        partial_value.astype(jnp.bfloat16), "tensor", scatter_dimension=0, tiled=True
    )
    expert_out = summed.reshape(slice_width, source_count, capacity)
    returned = lax.all_to_all(expert_out, "expert", split_axis=1, concat_axis=1, tiled=True)
    flat_back = returned.reshape(slice_width, expert_count * capacity)
    picked = jnp.take(flat_back, places, axis=1).astype(jnp.float32)
    weighted = picked * route_gates.reshape(-1)[None, :]
    combined = jnp.sum(weighted.reshape(slice_width, token_count, route_count), axis=2)
    return combined.T.astype(jnp.bfloat16)


ANY = pl.BlockSpec(memory_space=pl.ANY)
HBM = pl.BlockSpec(memory_space=pltpu.HBM)
VMEM = pl.BlockSpec(memory_space=pltpu.VMEM)
SMEM = pl.BlockSpec(memory_space=pltpu.SMEM)


def limit(size):
    return pltpu.CompilerParams(vmem_limit_bytes=size * 1024 * 1024)


def x_copies(parts, x_refs, x_all, sems, width):
    copies = []
    for i, block in enumerate(parts):
        for group, (number, first) in enumerate(block):
            rows = x_all.shape[0] // len(block)
            copies.append(
                pltpu.make_async_copy(
                    x_refs[number].at[pl.ds(first, rows), pl.ds(0, width)],
                    x_all.at[pl.ds(group * rows, rows), pl.ds(i * width, width)],
                    sems.at[i, group],
                )
            )
    return copies


def w_copies(blocks, depth, place, refs, w_all, sems, width):
    copies = [[] for _ in range(4)]
    for i, block in enumerate(blocks):
        source = lax.rem(place - block + depth, depth)
        rows = pl.ds(pl.multiple_of(source * width, width), width)
        for k in range(4):
            origin = refs[k].at[rows, :]
            copies[k].append(
                pltpu.make_async_copy(
                    origin, w_all.at[k, pl.ds(i * width, width), :], sems.at[k, i]
                )
            )
    return copies


def pick(x_all, picks_ref, xc_all, groups, columns):
    rows = x_all.shape[0] // groups
    slots = picks_ref.shape[1] // 2
    for group in range(groups):
        x = x_all[pl.ds(group * rows, rows), columns]
        z = jnp.dot(picks_ref[group], x, preferred_element_type=jnp.float32)
        z = z.astype(jnp.bfloat16)
        for expert in range(2):
            xc_all[expert, pl.ds(group * slots, slots), columns] = z[
                expert * slots : (expert + 1) * slots
            ]


def project_kernel(depth, blocks, parts, arrays, place_ref, *refs):
    x_refs, refs = refs[:arrays], refs[arrays:]
    w_refs, picks_ref, refs = refs[:4], refs[4], refs[5:]
    totals_refs, (x_all, xc_all, w_all, x_sems, w_sems) = refs[:4], refs[4:]
    groups = len(parts[0])
    width = x_all.shape[1] // len(blocks)
    xs = x_copies(parts, x_refs, x_all, x_sems, width)
    ws = w_copies(blocks, depth, place_ref[0], w_refs, w_all, w_sems, width)
    for copy in xs + ws[0] + ws[1] + ws[2] + ws[3]:
        copy.start()
    for i in range(len(blocks)):
        for copy in xs[i * groups : (i + 1) * groups]:
            copy.wait()
        pick(x_all, picks_ref, xc_all, groups, pl.ds(i * width, width))
    for k in range(4):
        for copy in ws[k]:
            copy.wait()
        totals_refs[k][...] = jnp.dot(
            xc_all[k // 2], w_all[k], preferred_element_type=jnp.float32
        )


def project(depth, place, blocks, arrays, parts, rows, width, weights, picks):
    half = weights[0].shape[1]
    groups = len(parts[0])
    total = rows * groups
    slots = groups * picks.shape[1] // 2
    span = len(blocks) * width
    return pl.pallas_call(
        functools.partial(project_kernel, depth, blocks, parts, len(arrays)),
        out_shape=[jax.ShapeDtypeStruct((slots, half), jnp.float32)] * 4,
        in_specs=[SMEM] + [ANY] * len(arrays) + [HBM] * 4 + [VMEM],
        out_specs=[VMEM] * 4,
        scratch_shapes=[
            pltpu.VMEM((total, span), jnp.bfloat16),
            pltpu.VMEM((2, slots, span), jnp.bfloat16),
            pltpu.VMEM((4, span, half), jnp.bfloat16),
            pltpu.SemaphoreType.DMA((len(blocks), groups)),
            pltpu.SemaphoreType.DMA((4, len(blocks))),
        ],
        compiler_params=limit(28),
        cost_estimate=pl.CostEstimate(
            flops=8 * total * span * half,
            bytes_accessed=8 * span * half + 16 * total * half,
            transcendentals=0,
        ),
    )(place, *arrays, *weights, picks)


def spread(hidden_ref, downs, places_ref, groups, put):
    slots = hidden_ref.shape[1] // groups
    each = [
        jnp.dot(hidden_ref[expert], downs[expert], preferred_element_type=jnp.float32).astype(
            jnp.bfloat16
        )
        for expert in range(2)
    ]
    for group in range(groups):
        part = slice(group * slots, (group + 1) * slots)
        both = jnp.concatenate([each[0][part], each[1][part]], axis=0)
        y = jnp.dot(places_ref[group], both, preferred_element_type=jnp.float32)
        put(group, y.astype(jnp.bfloat16))


def finish_kernel(depth, block, last, parts, arrays, place_ref, *refs):
    x_refs, refs = refs[:arrays], refs[arrays:]
    w_refs, down_refs, refs = refs[:4], refs[4:6], refs[6:]
    totals_refs, coef_ref, picks_ref, places_ref, refs = refs[:4], *refs[4:7], refs[7:]
    groups = len(parts[0])
    hidden_ref, y_refs, refs = refs[0], refs[1 : 1 + groups], refs[1 + groups :]
    x_all, xc_all, w_all, d_all, x_sems, w_sems, d_sems = refs
    width = x_all.shape[1]
    place = place_ref[0]
    xs = x_copies(parts, x_refs, x_all, x_sems, width)
    ws = w_copies([block], depth, place, w_refs, w_all, w_sems, width)
    target = lax.rem(place + last, depth)
    ds = [
        pltpu.make_async_copy(
            down_refs[k].at[:, pl.ds(pl.multiple_of(target * width, width), width)],
            d_all.at[k],
            d_sems.at[k],
        )
        for k in range(2)
    ]
    for copy in xs + ws[0] + ws[1] + ws[2] + ws[3] + ds:
        copy.start()
    for copy in xs:
        copy.wait()
    pick(x_all, picks_ref, xc_all, groups, pl.ds(0, width))
    for expert in range(2):
        for copy in ws[2 * expert] + ws[2 * expert + 1]:
            copy.wait()
        gate, up = [
            totals_refs[j][...]
            + jnp.dot(xc_all[expert], w_all[j], preferred_element_type=jnp.float32)
            for j in (2 * expert, 2 * expert + 1)
        ]
        value = gate / (1.0 + jnp.exp(-gate)) * up * coef_ref[:, expert : expert + 1]
        hidden_ref[expert] = value.astype(jnp.bfloat16)
    for copy in ds:
        copy.wait()

    def put(group, y):
        y_refs[group][...] = y

    spread(hidden_ref, d_all, places_ref, groups, put)


def finish(
    depth, place, block, last, arrays, parts, rows, width, weights, downs, totals, coef, picks, places
):
    half = weights[0].shape[1]
    groups = len(parts[0])
    total = groups * rows
    slots = groups * picks.shape[1] // 2
    outs = pl.pallas_call(
        functools.partial(finish_kernel, depth, block, last, parts, len(arrays)),
        out_shape=[jax.ShapeDtypeStruct((2, slots, half), jnp.bfloat16)]
        + [jax.ShapeDtypeStruct((rows, width), jnp.bfloat16)] * groups,
        in_specs=[SMEM] + [ANY] * len(arrays) + [HBM] * 6 + [VMEM] * 7,
        out_specs=[VMEM] * (1 + groups),
        scratch_shapes=[
            pltpu.VMEM((total, width), jnp.bfloat16),
            pltpu.VMEM((2, slots, width), jnp.bfloat16),
            pltpu.VMEM((4, width, half), jnp.bfloat16),
            pltpu.VMEM((2, half, width), jnp.bfloat16),
            pltpu.SemaphoreType.DMA((1, groups)),
            pltpu.SemaphoreType.DMA((4, 1)),
            pltpu.SemaphoreType.DMA((2,)),
        ],
        compiler_params=limit(28),
        cost_estimate=pl.CostEstimate(
            flops=12 * total * width * half,
            bytes_accessed=12 * width * half + 16 * total * half,
            transcendentals=2 * total * half,
        ),
    )(place, *arrays, *weights, *downs, *totals, coef, picks, places)
    return outs[0], outs[1:]


def descend_kernel(depth, blocks, groups, place_ref, hidden_ref, own_ref, other_ref, *refs):
    places_ref, refs = refs[0], refs[1:]
    y_refs, (d_all, sems) = refs[: groups * len(blocks)], refs[groups * len(blocks) :]
    width = d_all.shape[3]
    place = place_ref[0]
    copies = []
    for i, block in enumerate(blocks):
        target = lax.rem(place + block, depth)
        copies.append(
            [
                pltpu.make_async_copy(
                    ref.at[:, pl.ds(pl.multiple_of(target * width, width), width)],
                    d_all.at[i, k],
                    sems.at[i, k],
                )
                for k, ref in enumerate((own_ref, other_ref))
            ]
        )
    for pair in copies:
        for copy in pair:
            copy.start()
    for i, pair in enumerate(copies):
        for copy in pair:
            copy.wait()

        def put(group, y):
            y_refs[i * groups + group][...] = y

        spread(hidden_ref, d_all.at[i], places_ref, groups, put)


def descend(depth, place, blocks, groups, hidden, own, other, places):
    rows = places.shape[1]
    total = groups * rows
    half = own.shape[0]
    width = own.shape[1] // depth
    outs = pl.pallas_call(
        functools.partial(descend_kernel, depth, blocks, groups),
        out_shape=[jax.ShapeDtypeStruct((rows, width), jnp.bfloat16)] * (groups * len(blocks)),
        in_specs=[SMEM, VMEM, HBM, HBM, VMEM],
        out_specs=[VMEM] * (groups * len(blocks)),
        scratch_shapes=[
            pltpu.VMEM((len(blocks), 2, half, width), jnp.bfloat16),
            pltpu.SemaphoreType.DMA((len(blocks), 2)),
        ],
        compiler_params=limit(20),
        cost_estimate=pl.CostEstimate(
            flops=4 * total * len(blocks) * width * half,
            bytes_accessed=4 * len(blocks) * width * half + 2 * total * len(blocks) * width,
            transcendentals=0,
        ),
    )(place, hidden, own, other, places)
    return [outs[i * groups : (i + 1) * groups] for i in range(len(blocks))]


def after(value, *earlier):
    return lax.optimization_barrier((value,) + earlier)[0]


def fixed(value):
    return pltpu.with_memory_space_constraint(value, pltpu.HBM)


class Window:
    def __init__(self, size):
        self.size = size
        self.done = []

    def __call__(self, move, value, *earlier):
        if len(self.done) >= self.size:
            earlier += (self.done[-self.size],)
        self.done.append(move(after(value, *earlier) if earlier else value))
        return self.done[-1]


def gather_plan(tokens, routes, route_gates, gate_weight, up_weight, down_weight):
    devices = lax.axis_size("expert")
    depth = lax.axis_size("tensor")
    me = lax.axis_index("expert")
    spot = lax.axis_index("tensor").astype(jnp.int32)
    place = spot.reshape(1)
    wide, narrow = jnp.float32, jnp.bfloat16
    rows, width = tokens.shape

    def over(value, which):
        pairs = [(i, i ^ (2 if i % 2 == which else 4)) for i in range(devices)]
        return lax.ppermute(value, "expert", pairs)

    def near(value):
        return over(value, 0)

    def far(value):
        return over(value, 1)

    def twin(value):
        return lax.ppermute(value, "expert", [(i, i ^ 1) for i in range(devices)])

    def shift(by):
        pairs = [(i, (i + by) % depth) for i in range(depth)]
        return lambda value: lax.ppermute(value, "tensor", pairs)

    named = routes[:, :, None] == jnp.arange(devices, dtype=jnp.int32)[None, None, :]
    gates = jnp.sum(jnp.where(named, route_gates[:, :, None], 0.0), axis=1)
    high = gates.astype(narrow)
    rest = gates - high.astype(wide)
    middle = rest.astype(narrow)
    low = (rest - middle.astype(wide)).astype(narrow)
    extra = jnp.concatenate(
        [high, middle, low, jnp.zeros((rows, 128 - 3 * devices), narrow)], axis=1
    )
    marked = jnp.concatenate([tokens, extra], axis=1)

    plane, line = Window(3), Window(2)
    mine = [gate_weight[0], up_weight[0], down_weight[0]]
    other = [twin(w) for w in mine]
    z1 = shift(1)(tokens)
    b0 = far(marked)
    g0 = near(b0)
    a0 = near(after(marked, g0))
    z3 = shift(3)(after(tokens, g0))
    z13 = after(jnp.concatenate([z1, z3], axis=0), a0, *other)
    b13 = far(z13)
    a13 = near(z13)
    z2 = shift(1)(after(z1, a0, *other))
    g1 = shift(1)(after(g0, z2))
    g3 = near(b13[rows:])
    b2 = far(z2)
    a2 = near(z2)
    weights = [fixed(w) for w in (mine[0], mine[1], other[0], other[1])]
    downs = [fixed(mine[2]), fixed(other[2])]
    def gates_of(value):
        parts = value[:, width : width + 3 * devices].astype(wide).reshape(rows, 3, devices)
        whole = jnp.sum(parts, axis=1)
        return jnp.concatenate(
            [
                lax.dynamic_slice_in_dim(whole, me, 1, axis=1),
                lax.dynamic_slice_in_dim(whole, me ^ 1, 1, axis=1),
            ],
            axis=1,
        )

    coef = jnp.stack([gates_of(v).T for v in (marked, a0, b0, g0)])
    routed = coef > 0.0
    earlier = jnp.arange(rows)[:, None] < jnp.arange(rows)[None, :]
    slot = jnp.dot(
        routed.reshape(-1, rows).astype(narrow),
        earlier.astype(narrow),
        preferred_element_type=wide,
    ).reshape(coef.shape)
    capacity = 2 * rows * routes.shape[1] // devices
    numbers = jnp.arange(capacity, dtype=jnp.int32).astype(wide)
    matches = (slot[:, :, None, :] == numbers[None, None, :, None]) & routed[:, :, None, :]
    picks = matches.reshape(4, 2 * capacity, rows).astype(narrow)
    places = jnp.swapaxes(picks, 1, 2)
    coef = jnp.sum(jnp.where(matches, coef[:, :, None, :], 0.0), axis=3)
    coef = jnp.swapaxes(coef, 1, 2).reshape(4 * capacity, 2)

    arrays = [marked, a0, b0, g0, z13, a13, b13, g1, g3]
    parts = [
        [(4, 0), (5, 0), (6, 0), (7, 0)],
        [(4, rows), (5, rows), (6, rows), (8, 0)],
        [(0, 0), (1, 0), (2, 0), (3, 0)],
    ]
    totals = project(
        depth, place, [1, 3, 0], arrays, parts, rows, width, weights, picks
    )
    g2 = near(b2)

    hidden, y2 = finish(
        depth, place, 2, 2, [z2, a2, b2, g2], [[(i, 0) for i in range(4)]], rows, width,
        weights, downs, totals, coef, picks, places,
    )
    y = {2: y2}
    for late in ([1, 3], [0]):
        parts = descend(depth, place, late, 4, hidden, *downs, places)
        for d, part in zip(late, parts):
            y[d] = part

    def plus(*values):
        total = values[0].astype(wide)
        for value in values[1:]:
            total = total + value.astype(wide)
        return total

    plane, line = Window(3), Window(2)
    pg2 = near(y[2][3])
    pa2 = near(y[2][1])
    zg1 = shift(1)(y[1][3])
    zg3 = shift(3)(y[3][3])
    pb2 = far(plus(y[2][2], pg2).astype(narrow))
    pa1 = near(after(y[1][1], pa2))
    pb1 = far(after(y[1][2], pa2))
    u2 = shift(1)(plus(y[2][0], pa2, pb2).astype(narrow))
    pa3 = near(y[3][1])
    pb3 = far(y[3][2])
    pg0 = near(plus(y[0][3], zg1, zg3).astype(narrow))
    pa0 = near(after(y[0][1], pg0))
    pb0 = far(plus(y[0][2], pg0).astype(narrow))
    t1 = shift(1)(plus(y[1][0], pa1, pb1, u2).astype(narrow))
    t3 = shift(3)(plus(y[3][0], pa3, pb3).astype(narrow))
    return plus(y[0][0], pa0, pb0, t1, t3).astype(narrow)


def solution(mesh):
    small = mesh.shape["expert"] == 8 and mesh.shape["tensor"] == 4
    return jax.shard_map(
        gather_plan if small else dispatch_plan,
        mesh=mesh,
        in_specs=(
            P("expert", "tensor"),
            P("expert", None),
            P("expert", None),
            P("expert", None, "tensor"),
            P("expert", None, "tensor"),
            P("expert", "tensor", None),
        ),
        out_specs=P("expert", "tensor"),
        check_vma=False,
    )
```
